128 devices in a mesh: ctx: 8 (over x_hi, z), tp: 8 (over y, x_lo), dp: 2 (over core).
Axes of the slice: x: 4 (x_hi: 2, x_lo: 2; x = x_hi * 2 + x_lo), y: 4, z: 4, core: 2. Of those that a mesh axis runs over, the one named last changes fastest.
Arguments:
- patches: bfloat16 [2, 4096, 1280], P('dp', 'ctx'), may hold values from -6 to 6
- window_ids: int32 [2, 4096], P('dp', 'ctx'), may hold values from 0 to 8191, as said below
- vit_gain: float32 [1280], replicated, may hold values from 0.1 to 1.9
- vit_qkv: bfloat16 [1280, 3, 1280], P(None, None, 'tp')
- vit_out: bfloat16 [1280, 1280], P('tp')
- merge_gain: float32 [1280], replicated, may hold values from 0.1 to 1.9
- merge_up: bfloat16 [5120, 5120], P(None, 'tp'), may hold values from -0.078125 to 0.078125
- merge_down: bfloat16 [5120, 8192], P('tp', ('ctx', 'dp')), may hold values from -0.078125 to 0.078125
- text_rows: bfloat16 [2, 4096, 8192], P('dp', 'ctx', 'tp'), may hold values from -6 to 6
- placeholders: int32 [2, 1024], P('dp', 'ctx'), may hold values from 0 to 4095, as said below
- segments: int32 [2, 4096], P('dp'), may hold values from 0 to 3, never falling along the last dimension, each value on 1 to 2048 neighbouring positions
- llm_gain: float32 [8192], replicated, may hold values from 0.1 to 1.9
- w_query: bfloat16 [8192, 4096], P(None, 'tp')
- w_keyval: bfloat16 [8192, 2, 1024], P(None, None, 'tp')
Outputs:
- attended: bfloat16 [2, 4096, 4096], P('dp', 'ctx', 'tp')
The draws below stay inside these ranges and needn't reach their ends.
Inputs may be any that keep to these rules, and one draw needn't show every extreme that they name: `window_ids`: ids never fall along a sample's patches; a window holds 1 to 112 consecutive patches and never crosses from one ctx index's 512 patches to the next; every such block of patches holds a window of exactly 112. `placeholders`: the positions of one sample are distinct. The 128 vision rows of one ctx index put at most 32 rows into the 512 positions of any one ctx index, and exactly 32 into one of them.
All inputs are finite; a program needn't handle non-finite values.
Results may differ from the reference program's by a relative error of at most 0.025.
Values may be sent and summed in bfloat16 or wider, within the bound.
A program may use at most 128 MiB of HBM per device.

```python
import math
import jax
import jax.numpy as jnp
import numpy as np
from jax import lax

D = 8192
VD = 1280
VH = 16
VHD = 80
KVH = 8
HD = 128
QPK = 4
WIN = 112
PATCH_DEV = 512
TOK_DEV = 512
MH = 5120
HQ = 32
PATCHES = 4096
M_DEV = 128
SEQ = 4096
CAP = 32
N_CTX = 8
N_DP = 2


def draw_window_ids(key, part):
    key = jax.random.fold_in(key, 11)
    block_count = N_DP * N_CTX
    run_count = PATCH_DEV // (WIN // 4) + 3
    lead_most = min(WIN, PATCH_DEV - WIN)

    def per_block(sub_key, block_index):
        key_lengths, key_lead = jax.random.split(sub_key)
        run_lengths = jax.random.randint(key_lengths, (run_count,), WIN // 4, WIN + 1)
        lead_length = jax.random.randint(key_lead, (), 0, lead_most + 1)
        run_index = jnp.arange(run_count)
        run_lengths = jnp.where(run_index == 0, lead_length, run_lengths)
        run_lengths = jnp.where(run_index == 1, WIN, run_lengths)
        run_ends = jnp.cumsum(run_lengths)
        inside = (jnp.arange(PATCH_DEV)[:, None] >= run_ends[None, :]).astype(jnp.int32)
        return block_index * PATCH_DEV + jnp.sum(inside, axis=1)
    result = jax.vmap(per_block)(jax.random.split(key, block_count), jnp.arange(block_count))
    return result.reshape(N_DP, N_CTX * PATCH_DEV).astype(jnp.int32)


def draw_placeholders(key, part):
    key = jax.random.fold_in(key, 12)
    span = TOK_DEV // N_CTX
    slot_count = N_CTX * CAP

    def per_source(sub_key, source):
        key_full, key_order, key_rows, key_offsets = jax.random.split(sub_key, 4)
        full_dest = jax.random.randint(key_full, (), 0, N_CTX)
        order = jax.random.permutation(key_order, slot_count)
        dest_of_slot = jnp.arange(slot_count) // CAP
        ranking = jnp.where(dest_of_slot == full_dest, order - slot_count, order)
        chosen = jnp.argsort(ranking)[:M_DEV]
        chosen = chosen[jax.random.permutation(key_rows, M_DEV)]
        dest = chosen // CAP
        rank = chosen % CAP
        offsets = jax.vmap(lambda one_key: jax.random.permutation(one_key, span)[:CAP])(jax.random.split(key_offsets, N_CTX))
        return dest * TOK_DEV + source * span + offsets[dest, rank]
    sources = jnp.tile(jnp.arange(N_CTX), N_DP)
    result = jax.vmap(per_source)(jax.random.split(key, N_DP * N_CTX), sources)
    return result.reshape(N_DP, N_CTX * M_DEV).astype(jnp.int32)


def draw_vit_qkv(key, part):
    key = jax.random.fold_in(key, 13)
    key_query, key_keys, key_values = jax.random.split(key, 3)
    scale = VD ** (-0.5)
    columns = VH * VHD
    query_part = jax.random.normal(key_query, (VD, columns), jnp.float32) * scale
    value_part = jax.random.normal(key_values, (VD, columns), jnp.float32) * scale
    noise = jax.random.normal(key_keys, (VD, columns), jnp.float32) * scale
    key_part = noise
    return jnp.stack([query_part, key_part, value_part], axis=1).astype(jnp.bfloat16)


def draw_vit_out(key, part):
    key = jax.random.fold_in(key, 16)
    scale = 6.0 * (VH * VHD) ** (-0.5)
    values = jax.random.normal(key, (VH * VHD, VD), jnp.float32) * scale
    return jnp.clip(values, -6.0 * scale, 6.0 * scale).astype(jnp.bfloat16)


def query_base(key):
    return jax.random.normal(key, (D, KVH * QPK * HD), jnp.float32) * D ** (-0.5)


def draw_w_query(key, part):
    shared = query_base(key)
    return shared.astype(jnp.bfloat16)


def draw_w_keyval(key, part):
    key = jax.random.fold_in(key, 15)
    key_keys, key_values = jax.random.split(key, 2)
    scale = D ** (-0.5)
    value_part = jax.random.normal(key_values, (D, KVH * HD), jnp.float32) * scale
    noise = jax.random.normal(key_keys, (D, KVH * HD), jnp.float32) * scale
    key_part = noise
    return jnp.stack([key_part, value_part], axis=1).astype(jnp.bfloat16)


def levels(stream_key, extent, cuts, least, top_value):
    def one(dim, blocks):
        heights = jax.random.uniform(jax.random.fold_in(jax.random.fold_in(stream_key, 6), dim), (blocks,), jnp.float32, least / len(cuts), top_value / len(cuts))
        return jnp.repeat(jnp.exp(heights), extent[dim] // blocks).reshape((-1,) + (1,) * (len(extent) - dim - 1))

    level = one(*cuts[0])
    for cut in cuts[1:]:
        level = level * one(*cut)
    return level


def split_up(amount, total, limit, skew):
    loads = [(1 << 20) // math.isqrt(rank ** skew) + 1 for rank in range(2, amount + 1)]
    rest, holding = total - limit - (amount - 1), [1] * (amount - 1)
    while rest > 0:
        movable = [i for i in range(amount - 1) if holding[i] < limit]
        mass, left = sum([loads[i] for i in movable]), rest
        for i in movable:
            addition = min(limit - holding[i], max(1, left * loads[i] // mass), rest)
            holding[i] = holding[i] + addition
            rest = rest - addition
    return np.array([limit] + holding)


def ragged_sizes(own_key, amount, total, reach, lean):
    if amount == 2:
        one = jax.random.randint(own_key, (), max(1, total - reach), min(reach, total - 1) + 1)
        return jnp.stack([one, total - one])
    sizes = jnp.asarray(split_up(amount, total, reach, lean), jnp.int32)
    pairs = (amount - 1) // 2
    source_of, sink = sizes[1:1 + 2 * pairs:2], sizes[2:2 + 2 * pairs:2]
    room = jnp.minimum(source_of - 1, reach - sink)
    shifted = jax.random.randint(jax.random.fold_in(own_key, 1), (pairs,), 0, 1 << 20) % (room + 1)
    sizes = sizes.at[1:1 + 2 * pairs:2].set(source_of - shifted).at[2:2 + 2 * pairs:2].set(sink + shifted)
    return sizes[jax.random.permutation(jax.random.fold_in(own_key, 2), amount)]


def scatter_about(stream_key, extent, width, reach, shards=(), kind=jnp.bfloat16):
    values = width * jax.random.normal(stream_key, extent, jnp.float32)
    if shards:
        values = values * levels(stream_key, extent, shards, -0.22, 0.18)
    return jnp.clip(values, -reach, reach).astype(kind)


def setup_inputs(seed: int = 0) -> dict:
    keys = jax.random.split(jax.random.key(seed), 15)
    return {
        "patches": scatter_about(keys[0], (N_DP, PATCHES, VD), 1.0, 6.0, ((0, 2), (1, 8))),
        "window_ids": draw_window_ids(jax.random.fold_in(keys[14], 71), 0),
        "vit_gain": jnp.clip(1.0 + 0.18 * jax.random.normal(keys[2], (VD,), jnp.float32), 0.1, 1.9),
        "vit_qkv": draw_vit_qkv(jax.random.fold_in(keys[14], 71), 0),
        "vit_out": draw_vit_out(jax.random.fold_in(keys[14], 71), 0),
        "merge_gain": jnp.clip(1.0 + 0.18 * jax.random.normal(keys[5], (VD,), jnp.float32), 0.1, 1.9),
        "merge_up": scatter_about(keys[6], (4 * VD, MH), (4 * VD) ** -0.5, 0.078125, ((1, 8),)),
        "merge_down": scatter_about(keys[7], (MH, D), MH ** -0.5, 0.078125, ((0, 8), (1, 16))),
        "text_rows": scatter_about(keys[8], (N_DP, SEQ, D), 1.0, 6.0, ((0, 2), (1, 8), (2, 8))),
        "placeholders": draw_placeholders(jax.random.fold_in(keys[14], 71), 0),
        "segments": jax.vmap(lambda own: jnp.searchsorted(jnp.cumsum(ragged_sizes(own, 4, SEQ, SEQ // 2, 0)), jnp.arange(SEQ), side="right"))(jax.random.split(keys[10], N_DP)).reshape((N_DP, SEQ)).astype(jnp.int32),
        "llm_gain": jnp.clip(1.0 + 0.18 * jax.random.normal(keys[11], (D,), jnp.float32), 0.1, 1.9),
        "w_query": draw_w_query(jax.random.fold_in(keys[14], 71), 0),
        "w_keyval": draw_w_keyval(jax.random.fold_in(keys[14], 71), 0),
    }


epsilon = 1e-06
masked = -1e+30

def rms_norm(values, gain):
    values = values.astype(jnp.float32)
    return values * lax.rsqrt(lax.optimization_barrier(jnp.mean(values * values, axis=-1, keepdims=True)) + epsilon) * gain

def encode(rows, window_of, vit_gain, vit_qkv, vit_out, merge_gain, merge_up, merge_down):
    row_count = rows.shape[0]
    normed = rms_norm(rows, vit_gain).astype(jnp.bfloat16)
    projected = jnp.dot(normed, vit_qkv.reshape(VD, 3 * VH * VHD), preferred_element_type=jnp.float32).astype(jnp.bfloat16)
    projected = projected.reshape(row_count // PATCH_DEV, PATCH_DEV, 3, VH, VHD)
    blocks_of = window_of.reshape(row_count // PATCH_DEV, PATCH_DEV)

    def window_block(operands):
        block_proj, block_ids = operands
        queries = block_proj[:, 0].astype(jnp.float32)
        key_rows = block_proj[:, 1].astype(jnp.float32)
        value_rows = block_proj[:, 2].astype(jnp.float32)
        scores = jnp.einsum('qhd,khd->hqk', queries, key_rows) * VHD ** (-0.5)
        same = (block_ids[:, None] == block_ids[None, :])[None]
        highest = lax.optimization_barrier(jnp.max(jnp.where(same, scores, masked), axis=-1, keepdims=True))
        weights = jnp.where(same, jnp.exp(scores - highest), 0.0)
        totals = lax.optimization_barrier(jnp.sum(weights, axis=-1, keepdims=True))
        rounded = weights.astype(jnp.bfloat16).astype(jnp.float32)
        mixed_heads = jnp.einsum('hqk,khd->hqd', rounded, value_rows) / totals
        return mixed_heads.transpose(1, 0, 2).reshape(PATCH_DEV, VH * VHD).astype(jnp.bfloat16)
    head_rows = lax.map(window_block, (projected, blocks_of)).reshape(row_count, VH * VHD)
    residual = rows.astype(jnp.float32) + jnp.dot(head_rows, vit_out, preferred_element_type=jnp.float32)
    merged = rms_norm(residual, merge_gain).astype(jnp.bfloat16).reshape(row_count // 4, 4 * VD)
    inner = jax.nn.gelu(jnp.dot(merged, merge_up, preferred_element_type=jnp.float32), approximate=False).astype(jnp.bfloat16)
    return jnp.dot(inner, merge_down, preferred_element_type=jnp.float32).astype(jnp.bfloat16)

def decode_layer(mixed, segment_ids, llm_gain, w_query, w_keyval):
    normed = rms_norm(mixed, llm_gain).astype(jnp.bfloat16)
    queries = jnp.dot(normed, w_query, preferred_element_type=jnp.float32).astype(jnp.bfloat16)
    queries = queries.reshape(SEQ, KVH, QPK, HD).transpose(1, 0, 2, 3)
    keyvals = jnp.dot(normed, w_keyval.reshape(D, 2 * KVH * HD), preferred_element_type=jnp.float32).astype(jnp.bfloat16)
    keyvals = keyvals.reshape(SEQ, 2, KVH, HD)
    key_heads = keyvals[:, 0].transpose(1, 0, 2)
    value_heads = keyvals[:, 1].transpose(1, 0, 2)
    positions = jnp.arange(SEQ, dtype=jnp.int32)
    block_rows = min(512, SEQ)

    def per_head(operands):
        head_queries, head_keys, head_values = operands
        key_float = head_keys.astype(jnp.float32)
        value_float = head_values.astype(jnp.float32)

        def per_block(first_row):
            query_block = lax.dynamic_slice_in_dim(head_queries, first_row, block_rows, 0).astype(jnp.float32)
            query_pos = first_row + jnp.arange(block_rows, dtype=jnp.int32)
            query_seg = lax.dynamic_slice_in_dim(segment_ids, first_row, block_rows, 0)
            allowed = (query_seg[:, None] == segment_ids[None, :]) & (positions[None, :] <= query_pos[:, None])
            scores = jnp.einsum('qid,kd->iqk', query_block, key_float) * HD ** (-0.5)
            highest = lax.optimization_barrier(jnp.max(jnp.where(allowed[None], scores, masked), axis=-1, keepdims=True))
            weights = jnp.where(allowed[None], jnp.exp(scores - highest), 0.0)
            totals = lax.optimization_barrier(jnp.sum(weights, axis=-1, keepdims=True))
            rounded = weights.astype(jnp.bfloat16).astype(jnp.float32)
            mixed_heads = jnp.einsum('iqk,kd->iqd', rounded, value_float) / totals
            return mixed_heads.transpose(1, 0, 2)
        starts = jnp.arange(SEQ // block_rows, dtype=jnp.int32) * block_rows
        return lax.map(per_block, starts).reshape(SEQ, QPK, HD)
    result = lax.map(per_head, (queries, key_heads, value_heads))
    return result.transpose(1, 0, 2, 3).reshape(SEQ, HQ * HD).astype(jnp.bfloat16)

def reference(patches, window_ids, vit_gain, vit_qkv, vit_out, merge_gain, merge_up, merge_down, text_rows, placeholders, segments, llm_gain, w_query, w_keyval):
    results = []
    for sample in range(N_DP):
        vision = encode(patches[sample], window_ids[sample], vit_gain, vit_qkv, vit_out, merge_gain, merge_up, merge_down)
        mixed = text_rows[sample].at[placeholders[sample]].set(vision)
        results.append(decode_layer(mixed, segments[sample], llm_gain, w_query, w_keyval))
    return jnp.stack(results)
```

```python
import jax
import jax.numpy as jnp
from jax import lax
from jax.experimental import pallas as pl
from jax.experimental.pallas import tpu as pltpu
from jax.sharding import PartitionSpec as P

VHD = 80
HD = 128
EPS = 1e-06
MASKED = -1e30
BF = jnp.bfloat16
F32 = jnp.float32
MESH = pl.DeviceIdType.MESH
NT = (((1,), (1,)), ((), ()))


def dot(a, b):
    return jnp.dot(a, b, preferred_element_type=F32)


def dot_nt(a, b):
    return lax.dot_general(a, b, NT, preferred_element_type=F32)


def encode_kernel(
    patches, window_row, vit_gain, qkv_t, vit_out, merge_gain, merge_up, merge_down,
    text, place_row, llm_gain, w_query, w_keyval,
    q_text, kv_text, q_slots, kv_vis, pos_all,
    text_all, up_v, wd_all, wq_v, wkv_v, normed, q_v, k_v, v_v, heads_v,
    rs_send, rs_recv, own_part, merge_f, merged, acc_up, inner,
    rs2_send, rs2_recv, own_part2, vis_all, acc_t, ss_t, acc_v, ss_v, slots_out, kv_own,
    loc, txt_s, txt_r, wd_s, wd_r, sib_s, sib_r, rs_s, rs_r, mg_s, mg_r, r2_s, r2_r,
    vs_s, vs_r, kt_s, kt_r, qs_s, qs_r, kv_s, kv_r, ps_s, ps_r,
):
    c = lax.axis_index("ctx")
    t = lax.axis_index("tp")
    d = lax.axis_index("dp")
    y = t // 2
    x = lax.rem(t, 2)

    def tp_at(i):
        return (c, lax.rem(t + i, 8), d)

    def ctx_at(i):
        return (lax.rem(c + i, 8), t, d)

    def grid_at(dy, dx):
        return (c, lax.rem(y + dy, 4) * 2 + lax.rem(x + dx, 2), d)

    sibling = (c, t, 1 - d)

    def remote(src, dst, ssem, rsem, dev):
        cp = pltpu.make_async_remote_copy(
            src_ref=src, dst_ref=dst, send_sem=ssem, recv_sem=rsem, device_id=dev, device_id_type=MESH
        )
        cp.start()
        return cp

    barrier = pltpu.get_barrier_semaphore()
    for i in range(1, 8):
        pl.semaphore_signal(barrier, inc=1, device_id=tp_at(i), device_id_type=MESH)
        pl.semaphore_signal(barrier, inc=1, device_id=ctx_at(i), device_id_type=MESH)
    pl.semaphore_signal(barrier, inc=1, device_id=sibling, device_id_type=MESH)

    own_wd = c * 2 + d
    loads = [
        pltpu.make_async_copy(merge_down, wd_all.at[own_wd], loc.at[0]),
        pltpu.make_async_copy(merge_up, up_v, loc.at[1]),
        pltpu.make_async_copy(text, text_all.at[0], loc.at[2]),
        pltpu.make_async_copy(w_query, wq_v, loc.at[3]),
        pltpu.make_async_copy(w_keyval, wkv_v, loc.at[4]),
    ]
    for cp in loads:
        cp.start()
    pl.semaphore_wait(barrier, 15)

    pos_copies = []
    pos_all[pl.ds(c, 1), :] = place_row[...]
    for i in range(1, 8):
        pos_copies.append(
            remote(place_row, pos_all.at[pl.ds(c, 1)], ps_s.at[i], ps_r.at[i], ctx_at(i))
        )

    slot_of = lambda dy, dx: text_all.at[dy * 2 + dx]
    half = text.shape[0] // 2
    lo, hi = pl.ds(0, half), pl.ds(half, half)
    txt = {}

    def text_send(name, src, dst, dev):
        n = len(txt)
        txt[name] = remote(src, dst, txt_s.at[n], txt_r.at[n], dev)

    text_send("x0", text, slot_of(0, 1), grid_at(0, 1))
    text_send("yp", text, slot_of(3, 0), grid_at(1, 0))
    text_send("ym", text, slot_of(1, 0), grid_at(3, 0))

    wd_copies = [None]
    for i in range(1, 8):
        wd_copies.append(
            remote(merge_down, wd_all.at[own_wd], wd_s.at[i], wd_r.at[i], ctx_at(i))
        )
    sib_copies = [remote(merge_down, wd_all.at[own_wd], sib_s.at[0], sib_r.at[0], sibling)]

    rows = patches.shape[0]
    step = 128

    @pl.loop(0, rows // step)
    def _(r):
        sl = pl.ds(pl.multiple_of(r * step, step), step)
        v = patches[sl, :].astype(F32)
        ms = jnp.mean(v * v, axis=-1, keepdims=True)
        n = (v * lax.rsqrt(ms + EPS) * vit_gain[...]).astype(BF)
        q_v[sl, :] = dot_nt(n, qkv_t[0:160, :]).astype(BF)
        k_v[sl, :] = dot_nt(n, qkv_t[160:320, :]).astype(BF)
        v_v[sl, :] = dot_nt(n, qkv_t[320:480, :]).astype(BF)

    @pl.loop(0, rows // step)
    def _(r):
        sl = pl.ds(pl.multiple_of(r * step, step), step)
        qb = q_v[sl, :]
        col = lax.broadcasted_iota(jnp.int32, (step, 160), 1)
        ids = jnp.transpose(jnp.broadcast_to(window_row[:, sl], (8, step)))[:, 0:1]
        same = ids == window_row[...]
        outs = []
        for h in range(2):
            mine = (col < VHD) if h == 0 else (col >= VHD)
            qh = jnp.where(mine, qb, jnp.zeros_like(qb))
            s = dot_nt(qh, k_v[...]) * VHD ** (-0.5)
            s = jnp.where(same, s, MASKED)
            w = jnp.where(same, jnp.exp(s - jnp.max(s, axis=-1, keepdims=True)), 0.0)
            tot = jnp.sum(w, axis=-1, keepdims=True)
            outs.append(dot(w.astype(BF), v_v[...]) / tot)
        heads_v[sl, :] = jnp.where(col < VHD, outs[0], outs[1]).astype(BF)

    rs_copies = [None]
    for i in list(range(1, 8)) + [0]:
        dst = lax.rem(t + i, 8)
        hb = heads_v[pl.ds(pl.multiple_of(dst * 64, 64), 64), :]
        part = dot(hb, vit_out[...])
        if i == 0:
            own_part[...] = part
        else:
            rs_send[i] = part.astype(BF)
            rs_copies.append(remote(rs_send.at[i], rs_recv.at[i], rs_s.at[i], rs_r.at[i], tp_at(i)))

    txt["x0"].wait_recv()
    text_send("xyp", slot_of(0, 1), slot_of(3, 1), grid_at(1, 0))
    text_send("xym", slot_of(0, 1), slot_of(1, 1), grid_at(3, 0))
    txt["yp"].wait_recv()
    text_send("f1", slot_of(3, 0).at[lo], slot_of(2, 0).at[lo], grid_at(1, 0))
    txt["ym"].wait_recv()
    text_send("f2", slot_of(1, 0).at[hi], slot_of(2, 0).at[hi], grid_at(3, 0))

    for cp in rs_copies[1:]:
        cp.wait_recv()
    own_rows = pl.ds(pl.multiple_of(t * 64, 64), 64)
    res = patches[own_rows, :].astype(F32) + own_part[...]
    for i in range(1, 8):
        res += rs_recv[i].astype(F32)
    ms = jnp.mean(res * res, axis=-1, keepdims=True)
    res = res * lax.rsqrt(ms + EPS) * merge_gain[...]
    for b in range(10):
        merge_f[b] = res[:, b * 128 : (b + 1) * 128]
    own_m = pl.ds(pl.multiple_of(t * 16, 16), 16)
    for j in range(4):
        for b in range(10):
            at = j * 1280 + b * 128
            merged[own_m, at : at + 128] = merge_f[b, pl.ds(j, 16, stride=4), :].astype(BF)
    mg_copies = []
    for i in range(1, 8):
        mg_copies.append(
            remote(merged.at[own_m], merged.at[own_m], mg_s.at[i], mg_r.at[i], tp_at(i))
        )

    for i in range(1, 8):
        wd_copies[i].wait_recv()
        src = wd_all.at[lax.rem(c + 8 - i, 8) * 2 + d]
        sib_copies.append(remote(src, src, sib_s.at[i], sib_r.at[i], sibling))

    txt["f1"].wait_recv()
    text_send("g1", slot_of(2, 0).at[lo], slot_of(2, 1).at[lo], grid_at(0, 1))
    txt["f2"].wait_recv()
    text_send("g2", slot_of(2, 0).at[hi], slot_of(2, 1).at[hi], grid_at(0, 1))

    for cp in mg_copies:
        cp.wait_recv()
    loads[1].wait()
    acc_up[...] = jnp.zeros_like(acc_up)

    @pl.loop(0, 4)
    def _(k):
        sl = pl.ds(pl.multiple_of(k * 1280, 1280), 1280)
        acc_up[...] += dot(merged[:, sl], up_v[sl, :])

    pre = acc_up[...]
    inner[...] = (0.5 * pre * (1.0 + lax.erf(pre * (0.5**0.5)))).astype(BF)

    loads[0].wait()
    for cp in sib_copies:
        cp.wait_recv()
    r2_copies = [None]
    for i in list(range(1, 8)) + [0]:
        dst = lax.rem(t + i, 8)
        for e in range(2):
            part = dot(inner[...], wd_all[dst * 2 + e])
            if i == 0:
                own_part2[:, e * 512 : (e + 1) * 512] = part
            else:
                rs2_send[i, :, e * 512 : (e + 1) * 512] = part.astype(BF)
        if i:
            r2_copies.append(
                remote(rs2_send.at[i], rs2_recv.at[i], r2_s.at[i], r2_r.at[i], tp_at(i))
            )
    for cp in r2_copies[1:]:
        cp.wait_recv()
    total = own_part2[...]
    for i in range(1, 8):
        total += rs2_recv[i].astype(F32)
    vis_all[0] = total.astype(BF)
    vs_copies = [None]
    for i in range(1, 8):
        vs_copies.append(remote(vis_all.at[0], vis_all.at[i], vs_s.at[i], vs_r.at[i], tp_at(i)))

    loads[2].wait()
    loads[3].wait()
    loads[4].wait()
    for n in ("xyp", "xym", "g1", "g2"):
        txt[n].wait_recv()

    def project(source, slot, block, acc, ss, row_count, chunk):
        feats = pl.ds(pl.multiple_of(block * 1024, 1024), 1024)
        gain = llm_gain[pl.ds(block, 1), :]

        @pl.loop(0, row_count // chunk)
        def _(r):
            sl = pl.ds(pl.multiple_of(r * chunk, chunk), chunk)
            v = source[slot, sl, :].astype(F32)
            sq = v * v
            part = sq[:, 0:128]
            for j in range(1, 8):
                part += sq[:, j * 128 : (j + 1) * 128]
            ss[sl, :] += part
            xb = (v * gain).astype(BF)
            acc[sl, 0:512] += dot(xb, wq_v[feats, :])
            acc[sl, 512:768] += dot(xb, wkv_v[feats, :])

    def inverse(ss):
        return lax.rsqrt(jnp.sum(ss, axis=-1, keepdims=True) * (1.0 / 8192) + EPS)

    acc_t[...] = jnp.zeros_like(acc_t)
    ss_t[...] = jnp.zeros_like(ss_t)

    @pl.loop(0, 8)
    def _(slot):
        block = lax.rem(y + slot // 2, 4) * 2 + lax.rem(x + lax.rem(slot, 2), 2)
        project(text_all, slot, block, acc_t, ss_t, 512, 256)

    @pl.loop(0, 4)
    def _(r):
        sl = pl.ds(pl.multiple_of(r * 128, 128), 128)
        inv = inverse(ss_t[sl, :])
        q_text[sl, :] = (acc_t[sl, 0:512] * inv).astype(BF)
        kv_text[0, sl, :] = (acc_t[sl, 512:768] * inv).astype(BF)

    kt_copies = []
    for j in range(1, 5):
        kt_copies.append(remote(kv_text.at[0], kv_text.at[j], kt_s.at[j], kt_r.at[j], ctx_at(j)))

    for cp in vs_copies[1:]:
        cp.wait_recv()
    acc_v[...] = jnp.zeros_like(acc_v)
    ss_v[...] = jnp.zeros_like(ss_v)

    @pl.loop(0, 8)
    def _(slot):
        project(vis_all, slot, lax.rem(t + 8 - slot, 8), acc_v, ss_v, 128, 128)

    inv = inverse(ss_v[...])
    kv_own[...] = (acc_v[:, 512:768] * inv).astype(BF)
    kv_copies = []
    for i in range(1, 8):
        kv_copies.append(remote(kv_own, kv_vis.at[c], kv_s.at[i], kv_r.at[i], ctx_at(i)))
    kv_vis[c] = kv_own[...]
    qv = (acc_v[:, 0:512] * inv).astype(BF)
    dest = place_row[...] // 512
    hit = lax.broadcasted_iota(jnp.int32, (8, 128), 0) == dest
    hit_f = hit.astype(F32)
    before = (
        lax.broadcasted_iota(jnp.int32, (128, 128), 0) < lax.broadcasted_iota(jnp.int32, (128, 128), 1)
    ).astype(F32).astype(BF)
    rank = jnp.sum(dot(hit_f.astype(BF), before) * hit_f, axis=0, keepdims=True)
    slot_row = dest * 32 + rank.astype(jnp.int32)
    pick = (lax.broadcasted_iota(jnp.int32, (256, 128), 0) == slot_row).astype(F32).astype(BF)
    slots_out[...] = dot(pick, qv).astype(BF)
    qs_copies = []
    for i in range(1, 8):
        sl = pl.ds(pl.multiple_of(lax.rem(c + i, 8) * 32, 32), 32)
        qs_copies.append(remote(slots_out.at[sl], q_slots.at[c], qs_s.at[i], qs_r.at[i], ctx_at(i)))
    q_slots[c] = slots_out[pl.ds(pl.multiple_of(c * 32, 32), 32), :]

    for cp in kt_copies + kv_copies + qs_copies + pos_copies:
        cp.wait_recv()
    for cp in (
        list(txt.values()) + wd_copies[1:] + sib_copies + rs_copies[1:] + mg_copies + r2_copies[1:]
        + vs_copies[1:] + kt_copies + kv_copies + qs_copies + pos_copies
    ):
        cp.wait_send()


def attend_kernel(
    q_text, kv_text, q_slots, kv_vis, pos_all, segments, out,
    place, expand, q_v, k_v, v_v, bias, m_v, l_v, acc,
):
    c = lax.axis_index("ctx")
    lanes = kv_vis.shape[1]
    own = pl.ds(pl.multiple_of(c * 512, 512), 512)
    pos = pos_all[...]
    hit = (pos // 512) == c
    hit_f = hit.astype(F32)
    before = (
        lax.broadcasted_iota(jnp.int32, (128, 128), 0) < lax.broadcasted_iota(jnp.int32, (128, 128), 1)
    ).astype(F32).astype(BF)
    rank = dot(hit_f.astype(BF), before).astype(jnp.int32)
    slot = jnp.where(hit, rank, -1)
    ones = jnp.ones((1024, 128), BF)

    def fill_place(base):
        for s in range(8):
            rows = lax.broadcasted_iota(jnp.int32, (512, lanes), 0) + base
            place[:, s * lanes : (s + 1) * lanes] = (rows == pos[s : s + 1, :]).astype(F32).astype(BF)

    for s in range(8):
        back = (lax.broadcasted_iota(jnp.int32, (32, lanes), 0) == slot[s : s + 1, :]).astype(F32)
        expand[s * lanes : (s + 1) * lanes, :] = dot(
            jnp.transpose(back).astype(BF), q_slots[s]
        ).astype(BF)
    seg_q = jnp.transpose(jnp.broadcast_to(segments[:, own], (8, 512)))[:, 0:1]

    for j in range(5):
        base = (c - j) * 512

        @pl.when(base >= 0)
        def _():
            fill_place(base)
            is_vis = dot(place[...], ones) > 0.5
            k_v[...] = jnp.where(
                is_vis, dot(place[...], kv_vis[:, :, 0:128].reshape(1024, 128)),
                kv_text[j, :, 0:128].astype(F32),
            ).astype(BF)
            v_v[...] = jnp.where(
                is_vis, dot(place[...], kv_vis[:, :, 128:256].reshape(1024, 128)),
                kv_text[j, :, 128:256].astype(F32),
            ).astype(BF)
            if j == 0:
                for h in range(4):
                    sl = slice(h * 128, (h + 1) * 128)
                    q_v[:, sl] = jnp.where(
                        is_vis, dot(place[...], expand[:, sl]), q_text[:, sl].astype(F32)
                    ).astype(BF)
            seg_k = segments[:, pl.ds(pl.multiple_of(base, 512), 512)]
            allowed = seg_q == seg_k
            if j == 0:
                allowed = allowed & (
                    lax.broadcasted_iota(jnp.int32, (512, 512), 1)
                    <= lax.broadcasted_iota(jnp.int32, (512, 512), 0)
                )
            bias[...] = jnp.where(allowed, 0.0, MASKED)

            @pl.loop(0, 16)
            def _(it):
                h = it // 4
                r = lax.rem(it, 4)
                sl = pl.ds(pl.multiple_of(r * 128, 128), 128)
                hl = pl.ds(pl.multiple_of(h * 128, 128), 128)
                s_ = dot_nt(q_v[sl, hl], k_v[...]) * HD ** (-0.5) + bias[sl, :]
                top = jnp.max(s_, axis=-1, keepdims=True)
                if j == 0:
                    w = jnp.exp(s_ - top)
                    m_v[h, sl, :] = jnp.broadcast_to(top, (128, 128))
                    l_v[h, sl, :] = jnp.broadcast_to(jnp.sum(w, axis=-1, keepdims=True), (128, 128))
                    acc[h, sl, :] = dot(w.astype(BF), v_v[...])
                else:
                    old = m_v[h, sl, :]
                    new = jnp.maximum(old, top)
                    alpha = jnp.exp(old - new)
                    w = jnp.exp(s_ - new[:, 0:1])
                    m_v[h, sl, :] = new
                    l_v[h, sl, :] = l_v[h, sl, :] * alpha + jnp.sum(w, axis=-1, keepdims=True)
                    acc[h, sl, :] = acc[h, sl, :] * alpha + dot(w.astype(BF), v_v[...])

    for h in range(4):
        out[:, h * 128 : (h + 1) * 128] = (acc[h] / l_v[h]).astype(BF)


def shards(
    patches, window_ids, vit_gain, vit_qkv, vit_out, merge_gain, merge_up, merge_down,
    text_rows, placeholders, segments, llm_gain, w_query, w_keyval,
):
    vm = pl.BlockSpec(memory_space=pltpu.VMEM)
    hbm = pl.BlockSpec(memory_space=pl.ANY)
    dma = pltpu.SemaphoreType.DMA
    sds = jax.ShapeDtypeStruct
    qkv_t = vit_qkv.transpose(1, 2, 0).reshape(480, 1280)
    encoded = pl.pallas_call(
        encode_kernel,
        out_shape=(
            sds((512, 512), BF), sds((5, 512, 256), BF), sds((8, 32, 512), BF),
            sds((8, 128, 256), BF), sds((8, 128), jnp.int32),
        ),
        in_specs=[vm, vm, vm, vm, vm, vm, hbm, hbm, hbm, vm, vm, hbm, hbm],
        out_specs=(vm, vm, vm, vm, vm),
        scratch_shapes=[
            pltpu.VMEM((8, 512, 1024), BF),
            pltpu.VMEM((5120, 640), BF),
            pltpu.VMEM((16, 640, 512), BF),
            pltpu.VMEM((8192, 512), BF),
            pltpu.VMEM((8192, 256), BF),
            pltpu.VMEM((8, 128), BF),
            pltpu.VMEM((512, 160), BF),
            pltpu.VMEM((512, 160), BF),
            pltpu.VMEM((512, 160), BF),
            pltpu.VMEM((512, 160), BF),
            pltpu.VMEM((8, 64, 1280), BF),
            pltpu.VMEM((8, 64, 1280), BF),
            pltpu.VMEM((64, 1280), F32),
            pltpu.VMEM((10, 64, 128), F32),
            pltpu.VMEM((128, 5120), BF),
            pltpu.VMEM((128, 640), F32),
            pltpu.VMEM((128, 640), BF),
            pltpu.VMEM((8, 128, 1024), BF),
            pltpu.VMEM((8, 128, 1024), BF),
            pltpu.VMEM((128, 1024), F32),
            pltpu.VMEM((8, 128, 1024), BF),
            pltpu.VMEM((512, 768), F32),
            pltpu.VMEM((512, 128), F32),
            pltpu.VMEM((128, 768), F32),
            pltpu.VMEM((128, 128), F32),
            pltpu.VMEM((256, 512), BF),
            pltpu.VMEM((128, 256), BF),
            dma((5,)), dma((9,)), dma((9,)),
        ] + [dma((8,))] * 20,
        compiler_params=pltpu.CompilerParams(
            collective_id=0, has_side_effects=True, vmem_limit_bytes=63 * 2**20
        ),
    )(
        patches[0], window_ids, vit_gain.reshape(1, 1280), qkv_t, vit_out,
        merge_gain.reshape(1, 1280), merge_up, merge_down, text_rows[0], placeholders,
        llm_gain.reshape(8, 1024), w_query, w_keyval.reshape(8192, 256),
    )
    out = pl.pallas_call(
        attend_kernel,
        out_shape=sds((512, 512), BF),
        in_specs=[vm] * 6,
        out_specs=vm,
        scratch_shapes=[
            pltpu.VMEM((512, 1024), BF),
            pltpu.VMEM((1024, 512), BF),
            pltpu.VMEM((512, 512), BF),
            pltpu.VMEM((512, 128), BF),
            pltpu.VMEM((512, 128), BF),
            pltpu.VMEM((512, 512), F32),
            pltpu.VMEM((4, 512, 128), F32),
            pltpu.VMEM((4, 512, 128), F32),
            pltpu.VMEM((4, 512, 128), F32),
        ],
        compiler_params=pltpu.CompilerParams(vmem_limit_bytes=40 * 2**20),
    )(*encoded, segments)
    return out[None]


def solution(mesh):
    in_specs = (
        P("dp", "ctx", None),
        P("dp", "ctx"),
        P(),
        P(None, None, "tp"),
        P("tp", None),
        P(),
        P(None, "tp"),
        P("tp", ("ctx", "dp")),
        P("dp", "ctx", "tp"),
        P("dp", "ctx"),
        P("dp", None),
        P(),
        P(None, "tp"),
        P(None, None, "tp"),
    )
    out_specs = P("dp", "ctx", "tp")
    return jax.shard_map(shards, mesh=mesh, in_specs=in_specs, out_specs=out_specs, check_vma=False)
```

```python
import jax
import jax.numpy as jnp
from jax import lax
from jax.experimental import pallas as pl
from jax.experimental.pallas import tpu as pltpu
from jax.sharding import PartitionSpec as P

VHD = 80
HD = 128
EPS = 1e-06
MASKED = -1e30
BF = jnp.bfloat16
F32 = jnp.float32
MESH = pl.DeviceIdType.MESH
NT = (((1,), (1,)), ((), ()))


def dot(a, b):
    return jnp.dot(a, b, preferred_element_type=F32)


def dot_nt(a, b):
    return lax.dot_general(a, b, NT, preferred_element_type=F32)


class Sent:
    def __init__(self, copy):
        self.copy = copy
        self.arrived = False

    def wait_recv(self):
        if not self.arrived:
            self.arrived = True
            self.copy.wait_recv()


def encode_kernel(
    patches, window_row, vit_gain, qkv_t, vit_out, merge_gain, merge_up, merge_down,
    text, place_row, llm_gain, w_query, w_keyval,
    q_text, kv_text, q_slots, kv_vis, pos_all,
    text_all, up_v, wd_all, wq_v, wkv_raw, wkv_f, wkv_v, q_v, k_v, v_v, heads_v,
    rs_send, rs_recv, own_part, merge_f, merged, acc_up, inner,
    rs2_send, rs2_recv, own_part2, vis_all, acc_t, ss_t, acc_v, ss_v, slots_out, kv_own,
    loc, txt_s, txt_r, sib_s, sib_r, rs_s, rs_r, mg_s, mg_r, wd_s, wd_r, r2_s, r2_r,
    vs_s, vs_r, kt_s, kt_r, qs_s, qs_r, kv_s, kv_r, ps_s, ps_r,
):
    c = lax.axis_index("ctx")
    t = lax.axis_index("tp")
    d = lax.axis_index("dp")
    y = t // 2
    x = lax.rem(t, 2)
    started = []

    def tp_at(i):
        return (c, lax.rem(t + i, 8), d)

    def ctx_at(i):
        return (lax.rem(c + i, 8), t, d)

    def grid_at(dy, dx):
        return (c, lax.rem(y + dy, 4) * 2 + lax.rem(x + dx, 2), d)

    sibling = (c, t, 1 - d)

    def remote(src, dst, ssem, rsem, dev):
        cp = pltpu.make_async_remote_copy(
            src_ref=src, dst_ref=dst, send_sem=ssem, recv_sem=rsem, device_id=dev, device_id_type=MESH
        )
        cp.start()
        started.append(Sent(cp))
        return started[-1]

    def finish():
        for cp in started:
            cp.wait_recv()
        for cp in started:
            cp.copy.wait_send()
        for cp in loads:
            cp.wait_recv()

    barrier = pltpu.get_barrier_semaphore()
    for i in range(1, 8):
        pl.semaphore_signal(barrier, inc=1, device_id=tp_at(i), device_id_type=MESH)
        pl.semaphore_signal(barrier, inc=1, device_id=ctx_at(i), device_id_type=MESH)
    pl.semaphore_signal(barrier, inc=1, device_id=sibling, device_id_type=MESH)
    loads = [
        Sent(pltpu.make_async_copy(merge_down, wd_all.at[c * 2 + d], loc.at[0])),
        Sent(pltpu.make_async_copy(merge_up, up_v, loc.at[1])),
        Sent(pltpu.make_async_copy(text, text_all.at[0], loc.at[2])),
        Sent(pltpu.make_async_copy(w_query, wq_v, loc.at[3])),
    ] + [
        Sent(pltpu.make_async_copy(w_keyval.at[pl.ds(k * 2048, 2048)], wkv_raw.at[k % 2], loc.at[4 + k % 2]))
        for k in range(8)
    ]
    for cp in loads[:6]:
        cp.copy.start()
    pl.semaphore_wait(barrier, 15)

    pos_copies = []
    pos_all[pl.ds(c, 1), :] = place_row[...]
    for i in range(1, 8):
        pos_copies.append(
            remote(place_row, pos_all.at[pl.ds(c, 1)], ps_s.at[i], ps_r.at[i], ctx_at(i))
        )

    slot_of = lambda dy, dx: text_all.at[dy * 2 + dx]
    half = text.shape[0] // 2
    lo, hi = pl.ds(0, half), pl.ds(half, half)
    txt = {}

    def text_send(name, src, dst, dev):
        n = len(txt)
        txt[name] = remote(src, dst, txt_s.at[n], txt_r.at[n], dev)

    text_send("x0", text, slot_of(0, 1), grid_at(0, 1))
    text_send("yp", text, slot_of(3, 0), grid_at(1, 0))
    text_send("ym", text, slot_of(1, 0), grid_at(3, 0))

    x_hi = c // 4
    z = lax.rem(c, 4)

    def z_at(i):
        return (x_hi * 4 + lax.rem(z + i, 4), t, d)

    def wd_block(ctx):
        return wd_all.at[ctx * 2 + d]

    partner = lax.rem(c + 4, 8)
    wd_copies = [remote(merge_down, wd_block(c), wd_s.at[0], wd_r.at[0], (partner, t, d))]
    for i in (1, 3, 2):
        wd_copies.append(remote(merge_down, wd_block(c), wd_s.at[i], wd_r.at[i], z_at(i)))
    sib_copies = [remote(merge_down, wd_block(c), sib_s.at[0], sib_r.at[0], sibling)]

    def to_sibling(n, ctx):
        sib_copies.append(remote(wd_block(ctx), wd_block(ctx), sib_s.at[n], sib_r.at[n], sibling))

    rows = patches.shape[0]
    step = 128

    @pl.loop(0, rows // step)
    def _(r):
        sl = pl.ds(pl.multiple_of(r * step, step), step)
        v = patches[sl, :].astype(F32)
        ms = jnp.mean(v * v, axis=-1, keepdims=True)
        n = (v * lax.rsqrt(ms + EPS) * vit_gain[...][None, :]).astype(BF)
        q_v[sl, :] = dot_nt(n, qkv_t[0:160, :]).astype(BF)
        k_v[sl, :] = dot_nt(n, qkv_t[160:320, :]).astype(BF)
        v_v[sl, :] = dot_nt(n, qkv_t[320:480, :]).astype(BF)

    @pl.loop(0, rows // step)
    def _(r):
        sl = pl.ds(pl.multiple_of(r * step, step), step)
        qb = q_v[sl, :]
        col = lax.broadcasted_iota(jnp.int32, (step, 160), 1)
        ids = jnp.transpose(jnp.broadcast_to(window_row[:, sl], (8, step)))[:, 0:1]
        same = ids == window_row[...]
        outs = []
        for h in range(2):
            mine = (col < VHD) if h == 0 else (col >= VHD)
            qh = jnp.where(mine, qb, jnp.zeros_like(qb))
            s = dot_nt(qh, k_v[...]) * VHD ** (-0.5)
            s = jnp.where(same, s, MASKED)
            w = jnp.where(same, jnp.exp(s - jnp.max(s, axis=-1, keepdims=True)), 0.0)
            tot = jnp.sum(w, axis=-1, keepdims=True)
            outs.append(dot(w.astype(BF), v_v[...]) / tot)
        heads_v[sl, :] = jnp.where(col < VHD, outs[0], outs[1]).astype(BF)

    rs_copies = [None]
    for i in list(range(1, 8)) + [0]:
        dst = lax.rem(t + i, 8)
        hb = heads_v[pl.ds(pl.multiple_of(dst * 64, 64), 64), :]
        part = dot(hb, vit_out[...])
        if i == 0:
            own_part[...] = part
        else:
            rs_send[i] = part.astype(BF)
            rs_copies.append(remote(rs_send.at[i], rs_recv.at[i], rs_s.at[i], rs_r.at[i], tp_at(i)))

    for k in range(8):
        loads[4 + k].wait_recv()
        wkv_f[...] = wkv_raw[k % 2].astype(F32)
        if k < 6:
            loads[6 + k].copy.start()
        sl = pl.ds(k * 1024, 1024)
        wkv_v[sl, 0:128] = wkv_f[pl.ds(0, 1024, stride=2), :].astype(BF)
        wkv_v[sl, 128:256] = wkv_f[pl.ds(1, 1024, stride=2), :].astype(BF)

    wd_copies[0].wait_recv()
    for n, i in enumerate((1, 3, 2)):
        wd_copies.append(remote(wd_block(partner), wd_block(partner), wd_s.at[4 + n], wd_r.at[4 + n], z_at(i)))
    to_sibling(1, partner)

    for cp in rs_copies[1:]:
        cp.wait_recv()
    own_rows = pl.ds(pl.multiple_of(t * 64, 64), 64)
    res = patches[own_rows, :].astype(F32) + own_part[...]
    for i in range(1, 8):
        res += rs_recv[i].astype(F32)
    ms = jnp.mean(res * res, axis=-1, keepdims=True)
    res = res * lax.rsqrt(ms + EPS) * merge_gain[...][None, :]
    for b in range(10):
        merge_f[b] = res[:, b * 128 : (b + 1) * 128]
    own_m = pl.ds(pl.multiple_of(t * 16, 16), 16)
    for j in range(4):
        for b in range(10):
            at = j * 1280 + b * 128
            merged[own_m, at : at + 128] = merge_f[b, pl.ds(j, 16, stride=4), :].astype(BF)
    mg_copies = []
    for i in range(1, 8):
        mg_copies.append(
            remote(merged.at[own_m], merged.at[own_m], mg_s.at[i], mg_r.at[i], tp_at(i))
        )

    loads[2].wait_recv()
    loads[3].wait_recv()
    def project(source, slot, block, acc, ss, row_count, chunk):
        feats = pl.ds(pl.multiple_of(block * 1024, 1024), 1024)
        gain = llm_gain[feats][None, :]

        @pl.loop(0, row_count // chunk)
        def _(r):
            sl = pl.ds(pl.multiple_of(r * chunk, chunk), chunk)
            v = source[slot, sl, :].astype(F32)
            sq = v * v
            part = sq[:, 0:128]
            for j in range(1, 8):
                part += sq[:, j * 128 : (j + 1) * 128]
            ss[sl, :] += part
            xb = (v * gain).astype(BF)
            acc[sl, 0:512] += dot(xb, wq_v[feats, :])
            acc[sl, 512:768] += dot(xb, wkv_v[feats, :])

    def inverse(ss):
        return lax.rsqrt(jnp.sum(ss, axis=-1, keepdims=True) * (1.0 / 8192) + EPS)

    def project_text(first, second):
        @pl.loop(0, 2)
        def _(n):
            slot = jnp.where(n == 0, first, second)
            block = lax.rem(y + slot // 2, 4) * 2 + lax.rem(x + lax.rem(slot, 2), 2)
            project(text_all, slot, block, acc_t, ss_t, 512, 256)

    acc_t[...] = jnp.zeros_like(acc_t)
    ss_t[...] = jnp.zeros_like(ss_t)
    txt["x0"].wait_recv()
    project_text(0, 1)

    for cp in mg_copies:
        cp.wait_recv()
    txt["yp"].wait_recv()
    text_send("f1", slot_of(3, 0).at[lo], slot_of(2, 0).at[lo], grid_at(1, 0))
    txt["ym"].wait_recv()
    text_send("f2", slot_of(1, 0).at[hi], slot_of(2, 0).at[hi], grid_at(3, 0))
    txt["x0"].wait_recv()
    text_send("xyp", slot_of(0, 1), slot_of(3, 1), grid_at(1, 0))
    text_send("xym", slot_of(0, 1), slot_of(1, 1), grid_at(3, 0))

    loads[1].wait_recv()
    acc_up[...] = jnp.zeros_like(acc_up)

    @pl.loop(0, 4)
    def _(k):
        sl = pl.ds(pl.multiple_of(k * 1280, 1280), 1280)
        acc_up[...] += dot(merged[:, sl], up_v[sl, :])

    pre = acc_up[...]
    inner[...] = (0.5 * pre * (1.0 + lax.erf(pre * (0.5**0.5)))).astype(BF)

    project_text(2, 6)
    txt["f1"].wait_recv()
    text_send("g1", slot_of(2, 0).at[lo], slot_of(2, 1).at[lo], grid_at(0, 1))
    txt["f2"].wait_recv()
    text_send("g2", slot_of(2, 0).at[hi], slot_of(2, 1).at[hi], grid_at(0, 1))
    for n, i in enumerate((1, 3, 2)):
        wd_copies[1 + n].wait_recv()
        to_sibling(2 + n, x_hi * 4 + lax.rem(z + 4 - i, 4))
    for n, i in enumerate((1, 3, 2)):
        wd_copies[4 + n].wait_recv()
        to_sibling(5 + n, (1 - x_hi) * 4 + lax.rem(z + 4 - i, 4))

    loads[0].wait_recv()
    for cp in sib_copies:
        cp.wait_recv()
    r2_copies = [None]
    for i in list(range(1, 8)) + [0]:
        dst = lax.rem(t + i, 8)
        for e in range(2):
            part = dot(inner[...], wd_all[dst * 2 + e])
            if i == 0:
                own_part2[:, e * 512 : (e + 1) * 512] = part
            else:
                rs2_send[i, :, e * 512 : (e + 1) * 512] = part.astype(BF)
        if i:
            r2_copies.append(
                remote(rs2_send.at[i], rs2_recv.at[i], r2_s.at[i], r2_r.at[i], tp_at(i))
            )

    for n in ("xyp", "xym", "g1", "g2"):
        txt[n].wait_recv()
    project_text(3, 7)
    project_text(4, 5)

    @pl.loop(0, 4)
    def _(r):
        sl = pl.ds(pl.multiple_of(r * 128, 128), 128)
        inv = inverse(ss_t[sl, :])
        q_text[sl, :] = (acc_t[sl, 0:512] * inv).astype(BF)
        kv_text[0, sl, :] = (acc_t[sl, 512:768] * inv).astype(BF)

    def kt_copy(j):
        return pltpu.make_async_remote_copy(
            src_ref=kv_text.at[0], dst_ref=kv_text.at[j], send_sem=kt_s.at[j], recv_sem=kt_r.at[j],
            device_id=ctx_at(j), device_id_type=MESH,
        )

    for j in range(1, 5):

        @pl.when(c + j < 8)
        def _():
            kt_copy(j).start()

    for cp in r2_copies[1:]:
        cp.wait_recv()
    total = own_part2[...]
    for i in range(1, 8):
        total += rs2_recv[i].astype(F32)
    vis_all[0] = total.astype(BF)
    vs_copies = [None]
    for i in range(1, 8):
        vs_copies.append(remote(vis_all.at[0], vis_all.at[i], vs_s.at[i], vs_r.at[i], tp_at(i)))

    for cp in vs_copies[1:]:
        cp.wait_recv()
    acc_v[...] = jnp.zeros_like(acc_v)
    ss_v[...] = jnp.zeros_like(ss_v)

    @pl.loop(0, 8)
    def _(slot):
        project(vis_all, slot, lax.rem(t + 8 - slot, 8), acc_v, ss_v, 128, 128)

    inv = inverse(ss_v[...])
    kv_own[...] = (acc_v[:, 512:768] * inv).astype(BF)
    kv_copies = []
    for i in range(1, 8):
        kv_copies.append(remote(kv_own, kv_vis.at[c], kv_s.at[i], kv_r.at[i], ctx_at(i)))
    kv_vis[c] = kv_own[...]
    qv = (acc_v[:, 0:512] * inv).astype(BF)
    dest = place_row[...] // 512
    hit = lax.broadcasted_iota(jnp.int32, (8, 128), 0) == dest
    hit_f = hit.astype(F32)
    before = (
        lax.broadcasted_iota(jnp.int32, (128, 128), 0) < lax.broadcasted_iota(jnp.int32, (128, 128), 1)
    ).astype(F32).astype(BF)
    rank = jnp.sum(dot(hit_f.astype(BF), before) * hit_f, axis=0, keepdims=True)
    slot_row = dest * 32 + rank.astype(jnp.int32)
    pick = (lax.broadcasted_iota(jnp.int32, (256, 128), 0) == slot_row).astype(F32).astype(BF)
    slots_out[...] = dot(pick, qv).astype(BF)
    qs_copies = []
    for i in range(1, 8):
        sl = pl.ds(pl.multiple_of(lax.rem(c + i, 8) * 32, 32), 32)
        qs_copies.append(remote(slots_out.at[sl], q_slots.at[c], qs_s.at[i], qs_r.at[i], ctx_at(i)))
    q_slots[c] = slots_out[pl.ds(pl.multiple_of(c * 32, 32), 32), :]

    for j in range(1, 5):

        @pl.when(c - j >= 0)
        def _():
            kt_copy(j).wait_recv()

        @pl.when(c + j < 8)
        def _():
            kt_copy(j).wait_send()

    finish()


def attend_kernel(
    q_text, kv_text, q_slots, kv_vis, pos_all, seg_s, segments, out,
    place, expand, q_v, k_v, v_v, m_v, l_v, acc,
):
    c = lax.axis_index("ctx")
    lanes = kv_vis.shape[1]
    own = pl.ds(pl.multiple_of(c * 512, 512), 512)
    pos = pos_all[...]
    hit = (pos // 512) == c
    before = (
        lax.broadcasted_iota(jnp.int32, (128, 128), 0) < lax.broadcasted_iota(jnp.int32, (128, 128), 1)
    ).astype(F32).astype(BF)
    rank = dot(hit.astype(F32).astype(BF), before).astype(jnp.int32)
    slot = jnp.where(hit, rank, -1)
    ones = jnp.ones((1024, 128), BF)

    for s in range(8):
        back = (lax.broadcasted_iota(jnp.int32, (32, lanes), 0) == slot[s : s + 1, :]).astype(F32)
        expand[s * lanes : (s + 1) * lanes, :] = dot(
            jnp.transpose(back).astype(BF), q_slots[s]
        ).astype(BF)
    seg_q = jnp.transpose(jnp.broadcast_to(segments[:, own], (8, 512)))[:, 0:1]
    log2e = 1.4426950408889634

    for j in range(5):
        base = (c - j) * 512
        first = jnp.maximum(base, 0)

        @pl.when((base >= 0) & (seg_s[0, first + 511] == seg_s[0, c * 512]) if j else base >= 0)
        def _():
            rows = lax.broadcasted_iota(jnp.int32, (512, lanes), 0) + base
            for s in range(8):
                place[:, s * lanes : (s + 1) * lanes] = (
                    (rows == pos[s : s + 1, :]).astype(F32).astype(BF)
                )
            is_vis = dot(place[...], ones) > 0.5
            placed = dot(place[...], kv_vis[...].reshape(1024, 256))
            k_v[...] = jnp.where(is_vis, placed[:, 0:128], kv_text[j, :, 0:128].astype(F32)).astype(BF)
            v_v[...] = jnp.where(is_vis, placed[:, 128:256], kv_text[j, :, 128:256].astype(F32)).astype(BF)
            if j == 0:
                placed_q = dot(place[...], expand[...])
                for h in range(4):
                    sl = slice(h * 128, (h + 1) * 128)
                    qh = jnp.where(is_vis, placed_q[:, sl], q_text[:, sl].astype(F32)).astype(BF)
                    for r in range(4):
                        q_v[r, sl, :] = qh[r * 128 : (r + 1) * 128, :]
            seg_k = segments[:, pl.ds(pl.multiple_of(first, 512), 512)]
            for r in range(4):
                wide = (r + 1) * 128 if j == 0 else 512
                allowed = seg_q[r * 128 : (r + 1) * 128] == seg_k[:, 0:wide]
                if j == 0:
                    allowed = allowed & (
                        lax.broadcasted_iota(jnp.int32, (128, wide), 1)
                        <= lax.broadcasted_iota(jnp.int32, (128, wide), 0) + r * 128
                    )
                bias = jnp.where(allowed, 0.0, MASKED)
                s_ = dot_nt(q_v[r], k_v[0:wide, :]) * (HD ** (-0.5) * log2e)
                s_ = (s_.reshape(4, 128, wide) + bias[None]).reshape(512, wide)
                top = jnp.max(s_, axis=-1, keepdims=True)
                if j == 0:
                    w = jnp.exp2(s_ - top)
                    m_v[r] = jnp.broadcast_to(top, (512, 128))
                    l_v[r] = jnp.broadcast_to(jnp.sum(w, axis=-1, keepdims=True), (512, 128))
                    acc[r] = dot(w.astype(BF), v_v[0:wide, :])
                else:
                    old = m_v[r]
                    new = jnp.maximum(old, top)
                    alpha = jnp.exp2(old - new)
                    w = jnp.exp2(s_ - new[:, 0:1])
                    m_v[r] = new
                    l_v[r] = l_v[r] * alpha + jnp.sum(w, axis=-1, keepdims=True)
                    acc[r] = acc[r] * alpha + dot(w.astype(BF), v_v[...])

    for r in range(4):
        for h in range(4):
            sl = slice(h * 128, (h + 1) * 128)
            out[r * 128 : (r + 1) * 128, sl] = (acc[r, sl, :] / l_v[r, sl, :]).astype(BF)


def shards(
    patches, window_ids, vit_gain, vit_qkv, vit_out, merge_gain, merge_up, merge_down,
    text_rows, placeholders, segments, llm_gain, w_query, w_keyval,
):
    vm = pl.BlockSpec(memory_space=pltpu.VMEM)
    hbm = pl.BlockSpec(memory_space=pl.ANY)
    dma = pltpu.SemaphoreType.DMA
    sds = jax.ShapeDtypeStruct
    qkv_t = vit_qkv.transpose(1, 2, 0).reshape(480, 1280)
    encoded = pl.pallas_call(
        encode_kernel,
        out_shape=(
            sds((512, 512), BF), sds((5, 512, 256), BF), sds((8, 32, 512), BF),
            sds((8, 128, 256), BF), sds((8, 128), jnp.int32),
        ),
        in_specs=[vm, vm, vm, vm, vm, vm, hbm, hbm, hbm, vm, vm, hbm, hbm],
        out_specs=(vm, vm, vm, vm, vm),
        scratch_shapes=[
            pltpu.VMEM((8, 512, 1024), BF),
            pltpu.VMEM((5120, 640), BF),
            pltpu.VMEM((16, 640, 512), BF),
            pltpu.VMEM((8192, 512), BF),
            pltpu.VMEM((2, 2048, 128), BF),
            pltpu.VMEM((2048, 128), F32),
            pltpu.VMEM((8192, 256), BF),
            pltpu.VMEM((512, 160), BF),
            pltpu.VMEM((512, 160), BF),
            pltpu.VMEM((512, 160), BF),
            pltpu.VMEM((512, 160), BF),
            pltpu.VMEM((8, 64, 1280), BF),
            pltpu.VMEM((8, 64, 1280), BF),
            pltpu.VMEM((64, 1280), F32),
            pltpu.VMEM((10, 64, 128), F32),
            pltpu.VMEM((128, 5120), BF),
            pltpu.VMEM((128, 640), F32),
            pltpu.VMEM((128, 640), BF),
            pltpu.VMEM((8, 128, 1024), BF),
            pltpu.VMEM((8, 128, 1024), BF),
            pltpu.VMEM((128, 1024), F32),
            pltpu.VMEM((8, 128, 1024), BF),
            pltpu.VMEM((512, 768), F32),
            pltpu.VMEM((512, 128), F32),
            pltpu.VMEM((128, 768), F32),
            pltpu.VMEM((128, 128), F32),
            pltpu.VMEM((256, 512), BF),
            pltpu.VMEM((128, 256), BF),
            dma((6,)), dma((9,)), dma((9,)),
        ] + [dma((8,))] * 20,
        compiler_params=pltpu.CompilerParams(
            collective_id=0, has_side_effects=True, vmem_limit_bytes=63 * 2**20
        ),
    )(
        patches[0], window_ids, vit_gain, qkv_t, vit_out,
        merge_gain, merge_up, merge_down, text_rows[0], placeholders,
        llm_gain, w_query, w_keyval.reshape(16384, 128),
    )
    out = pl.pallas_call(
        attend_kernel,
        out_shape=sds((512, 512), BF),
        in_specs=[vm] * 5 + [pl.BlockSpec(memory_space=pltpu.SMEM), vm],
        out_specs=vm,
        scratch_shapes=[
            pltpu.VMEM((512, 1024), BF),
            pltpu.VMEM((1024, 512), BF),
            pltpu.VMEM((4, 512, 128), BF),
            pltpu.VMEM((512, 128), BF),
            pltpu.VMEM((512, 128), BF),
            pltpu.VMEM((4, 512, 128), F32),
            pltpu.VMEM((4, 512, 128), F32),
            pltpu.VMEM((4, 512, 128), F32),
        ],
        compiler_params=pltpu.CompilerParams(vmem_limit_bytes=60 * 2**20),
    )(*encoded, segments, segments)
    return out[None]


def solution(mesh):
    in_specs = (
        P("dp", "ctx", None),
        P("dp", "ctx"),
        P(),
        P(None, None, "tp"),
        P("tp", None),
        P(),
        P(None, "tp"),
        P("tp", ("ctx", "dp")),
        P("dp", "ctx", "tp"),
        P("dp", "ctx"),
        P("dp", None),
        P(),
        P(None, "tp"),
        P(None, None, "tp"),
    )
    out_specs = P("dp", "ctx", "tp")
    return jax.shard_map(shards, mesh=mesh, in_specs=in_specs, out_specs=out_specs, check_vma=False)
```

```python
import jax
import jax.numpy as jnp
from jax import lax
from jax.experimental import pallas as pl
from jax.experimental.pallas import tpu as pltpu
from jax.sharding import PartitionSpec as P

VHD = 80
HD = 128
EPS = 1e-06
MASKED = -1e30
BF = jnp.bfloat16
F32 = jnp.float32
MESH = pl.DeviceIdType.MESH
NT = (((1,), (1,)), ((), ()))


def dot(a, b):
    return jnp.dot(a, b, preferred_element_type=F32)


def dot_nt(a, b):
    return lax.dot_general(a, b, NT, preferred_element_type=F32)


class Sent:
    def __init__(self, copy):
        self.copy = copy
        self.arrived = False

    def wait_recv(self):
        if not self.arrived:
            self.arrived = True
            self.copy.wait_recv()


def encode_kernel(
    patches, window_row, vit_gain, qkv_t, vit_out, merge_gain, merge_up, merge_down,
    text, place_row, llm_gain, w_query, w_keyval,
    q_text, kv_text, q_slots, kv_vis, pos_all,
    text_all, up_v, wd_all, wq_v, wkv_raw, wkv_f, wkv_v, q_v, k_v, v_v, heads_v,
    rs_send, rs_recv, own_part, merge_f, merged, acc_up, inner,
    rs2_send, rs2_recv, own_part2, vis_all, acc_t, ss_t, acc_v, ss_v, slots_out, kv_own,
    loc, txt_s, txt_r, sib_s, sib_r, rs_s, rs_r, mg_s, mg_r, wd_s, wd_r, r2_s, r2_r,
    vs_s, vs_r, kt_s, kt_r, qs_s, qs_r, kv_s, kv_r, ps_s, ps_r,
):
    c = lax.axis_index("ctx")
    t = lax.axis_index("tp")
    d = lax.axis_index("dp")
    y = t // 2
    x = lax.rem(t, 2)
    started = []

    def tp_at(i):
        return (c, lax.rem(t + i, 8), d)

    def ctx_at(i):
        return (lax.rem(c + i, 8), t, d)

    def grid_at(dy, dx):
        return (c, lax.rem(y + dy, 4) * 2 + lax.rem(x + dx, 2), d)

    sibling = (c, t, 1 - d)

    def remote(src, dst, ssem, rsem, dev):
        cp = pltpu.make_async_remote_copy(
            src_ref=src, dst_ref=dst, send_sem=ssem, recv_sem=rsem, device_id=dev, device_id_type=MESH
        )
        cp.start()
        started.append(Sent(cp))
        return started[-1]

    def finish():
        for cp in started:
            cp.wait_recv()
        for cp in started:
            cp.copy.wait_send()
        for cp in loads:
            cp.wait_recv()

    barrier = pltpu.get_barrier_semaphore()
    for i in range(1, 8):
        pl.semaphore_signal(barrier, inc=1, device_id=tp_at(i), device_id_type=MESH)
        pl.semaphore_signal(barrier, inc=1, device_id=ctx_at(i), device_id_type=MESH)
    pl.semaphore_signal(barrier, inc=1, device_id=sibling, device_id_type=MESH)
    loads = [
        Sent(pltpu.make_async_copy(merge_down, wd_all.at[c * 2 + d], loc.at[0])),
        Sent(pltpu.make_async_copy(merge_up, up_v, loc.at[1])),
        Sent(pltpu.make_async_copy(text, text_all.at[0], loc.at[2])),
        Sent(pltpu.make_async_copy(w_query, wq_v, loc.at[3])),
    ] + [
        Sent(pltpu.make_async_copy(w_keyval.at[pl.ds(k * 2048, 2048)], wkv_raw.at[k % 2], loc.at[4 + k % 2]))
        for k in range(8)
    ]
    for cp in loads[:6]:
        cp.copy.start()
    pl.semaphore_wait(barrier, 15)

    pos_copies = []
    pos_all[pl.ds(c, 1), :] = place_row[...]
    for i in range(1, 8):
        pos_copies.append(
            remote(place_row, pos_all.at[pl.ds(c, 1)], ps_s.at[i], ps_r.at[i], ctx_at(i))
        )

    slot_of = lambda dy, dx: text_all.at[dy * 2 + dx]
    half = text.shape[0] // 2
    lo, hi = pl.ds(0, half), pl.ds(half, half)
    txt = {}

    def text_send(name, src, dst, dev):
        n = len(txt)
        txt[name] = remote(src, dst, txt_s.at[n], txt_r.at[n], dev)

    text_send("x0", text, slot_of(0, 1), grid_at(0, 1))
    text_send("yp", text, slot_of(3, 0), grid_at(1, 0))
    text_send("ym", text, slot_of(1, 0), grid_at(3, 0))

    x_hi = c // 4
    z = lax.rem(c, 4)

    def z_at(i):
        return (x_hi * 4 + lax.rem(z + i, 4), t, d)

    def wd_block(ctx):
        return wd_all.at[ctx * 2 + d]

    partner = lax.rem(c + 4, 8)
    wd_copies = [remote(merge_down, wd_block(c), wd_s.at[0], wd_r.at[0], (partner, t, d))]
    for i in (1, 3, 2):
        wd_copies.append(remote(merge_down, wd_block(c), wd_s.at[i], wd_r.at[i], z_at(i)))
    sib_copies = [remote(merge_down, wd_block(c), sib_s.at[0], sib_r.at[0], sibling)]

    def to_sibling(n, ctx):
        sib_copies.append(remote(wd_block(ctx), wd_block(ctx), sib_s.at[n], sib_r.at[n], sibling))

    rows = patches.shape[0]
    step = 128

    @pl.loop(0, rows // step)
    def _(r):
        sl = pl.ds(pl.multiple_of(r * step, step), step)
        v = patches[sl, :].astype(F32)
        ms = jnp.mean(v * v, axis=-1, keepdims=True)
        n = (v * lax.rsqrt(ms + EPS) * vit_gain[...][None, :]).astype(BF)
        q_v[sl, :] = dot_nt(n, qkv_t[0:160, :]).astype(BF)
        k_v[sl, :] = dot_nt(n, qkv_t[160:320, :]).astype(BF)
        v_v[sl, :] = dot_nt(n, qkv_t[320:480, :]).astype(BF)

    @pl.loop(0, rows // step)
    def _(r):
        sl = pl.ds(pl.multiple_of(r * step, step), step)
        qb = q_v[sl, :]
        col = lax.broadcasted_iota(jnp.int32, (step, 160), 1)
        ids = jnp.transpose(jnp.broadcast_to(window_row[:, sl], (8, step)))[:, 0:1]
        same = ids == window_row[...]
        outs = []
        for h in range(2):
            mine = (col < VHD) if h == 0 else (col >= VHD)
            qh = jnp.where(mine, qb, jnp.zeros_like(qb))
            s = dot_nt(qh, k_v[...]) * VHD ** (-0.5)
            s = jnp.where(same, s, MASKED)
            w = jnp.where(same, jnp.exp(s - jnp.max(s, axis=-1, keepdims=True)), 0.0)
            tot = jnp.sum(w, axis=-1, keepdims=True)
            outs.append(dot(w.astype(BF), v_v[...]) / tot)
        heads_v[sl, :] = jnp.where(col < VHD, outs[0], outs[1]).astype(BF)

    rs_copies = [None]
    for i in list(range(1, 8)) + [0]:
        dst = lax.rem(t + i, 8)
        hb = heads_v[pl.ds(pl.multiple_of(dst * 64, 64), 64), :]
        part = dot(hb, vit_out[...])
        if i == 0:
            own_part[...] = part
        else:
            rs_send[i] = part.astype(BF)
            rs_copies.append(remote(rs_send.at[i], rs_recv.at[i], rs_s.at[i], rs_r.at[i], tp_at(i)))

    for k in range(8):
        loads[4 + k].wait_recv()
        wkv_f[...] = wkv_raw[k % 2].astype(F32)
        if k < 6:
            loads[6 + k].copy.start()
        sl = pl.ds(k * 1024, 1024)
        wkv_v[sl, 0:128] = wkv_f[pl.ds(0, 1024, stride=2), :].astype(BF)
        wkv_v[sl, 128:256] = wkv_f[pl.ds(1, 1024, stride=2), :].astype(BF)

    wd_copies[0].wait_recv()
    for n, i in enumerate((1, 3, 2)):
        wd_copies.append(remote(wd_block(partner), wd_block(partner), wd_s.at[4 + n], wd_r.at[4 + n], z_at(i)))
    to_sibling(1, partner)

    for cp in rs_copies[1:]:
        cp.wait_recv()
    own_rows = pl.ds(pl.multiple_of(t * 64, 64), 64)
    res = patches[own_rows, :].astype(F32) + own_part[...]
    for i in range(1, 8):
        res += rs_recv[i].astype(F32)
    ms = jnp.mean(res * res, axis=-1, keepdims=True)
    res = res * lax.rsqrt(ms + EPS) * merge_gain[...][None, :]
    for b in range(10):
        merge_f[b] = res[:, b * 128 : (b + 1) * 128]
    own_m = pl.ds(pl.multiple_of(t * 16, 16), 16)
    for j in range(4):
        for b in range(10):
            at = j * 1280 + b * 128
            merged[own_m, at : at + 128] = merge_f[b, pl.ds(j, 16, stride=4), :].astype(BF)
    def merged_at(dy, dx, cols=slice(None)):
        block = lax.rem(y + dy, 4) * 2 + lax.rem(x + dx, 2)
        return merged.at[pl.ds(pl.multiple_of(block * 16, 16), 16), cols]

    mrg = {}

    def merged_send(name, ref, dev):
        n = len(mrg)
        mrg[name] = remote(ref, ref, mg_s.at[n], mg_r.at[n], dev)

    left, right = pl.ds(0, 2560), pl.ds(2560, 2560)
    merged_send("yp", merged_at(0, 0), grid_at(1, 0))
    merged_send("ym", merged_at(0, 0), grid_at(3, 0))
    merged_send("x0", merged_at(0, 0), grid_at(0, 1))
    mrg["yp"].wait_recv()
    merged_send("f1", merged_at(3, 0, left), grid_at(1, 0))
    mrg["ym"].wait_recv()
    merged_send("f2", merged_at(1, 0, right), grid_at(3, 0))
    mrg["x0"].wait_recv()
    merged_send("xyp", merged_at(0, 1), grid_at(1, 0))
    merged_send("xym", merged_at(0, 1), grid_at(3, 0))
    mrg["f1"].wait_recv()
    merged_send("g1", merged_at(2, 0, left), grid_at(0, 1))
    mrg["f2"].wait_recv()
    merged_send("g2", merged_at(2, 0, right), grid_at(0, 1))

    loads[2].wait_recv()
    loads[3].wait_recv()
    def project(source, slot, block, acc, ss, row_count, chunk):
        feats = pl.ds(pl.multiple_of(block * 1024, 1024), 1024)
        gain = llm_gain[feats][None, :]

        @pl.loop(0, row_count // chunk)
        def _(r):
            sl = pl.ds(pl.multiple_of(r * chunk, chunk), chunk)
            v = source[slot, sl, :].astype(F32)
            sq = v * v
            part = sq[:, 0:128]
            for j in range(1, 8):
                part += sq[:, j * 128 : (j + 1) * 128]
            ss[sl, :] += part
            xb = (v * gain).astype(BF)
            acc[sl, 0:512] += dot(xb, wq_v[feats, :])
            acc[sl, 512:768] += dot(xb, wkv_v[feats, :])

    def inverse(ss):
        return lax.rsqrt(jnp.sum(ss, axis=-1, keepdims=True) * (1.0 / 8192) + EPS)

    def project_text(first, second):
        @pl.loop(0, 2)
        def _(n):
            slot = jnp.where(n == 0, first, second)
            block = lax.rem(y + slot // 2, 4) * 2 + lax.rem(x + lax.rem(slot, 2), 2)
            project(text_all, slot, block, acc_t, ss_t, 512, 256)

    acc_t[...] = jnp.zeros_like(acc_t)
    ss_t[...] = jnp.zeros_like(ss_t)
    txt["x0"].wait_recv()
    project_text(0, 1)

    for cp in mrg.values():
        cp.wait_recv()
    txt["yp"].wait_recv()
    text_send("f1", slot_of(3, 0).at[lo], slot_of(2, 0).at[lo], grid_at(1, 0))
    txt["ym"].wait_recv()
    text_send("f2", slot_of(1, 0).at[hi], slot_of(2, 0).at[hi], grid_at(3, 0))
    loads[1].wait_recv()
    acc_up[...] = jnp.zeros_like(acc_up)

    @pl.loop(0, 4)
    def _(k):
        sl = pl.ds(pl.multiple_of(k * 1280, 1280), 1280)
        acc_up[...] += dot(merged[:, sl], up_v[sl, :])

    pre = acc_up[...]
    inner[...] = (0.5 * pre * (1.0 + lax.erf(pre * (0.5**0.5)))).astype(BF)

    project_text(2, 6)
    txt["f1"].wait_recv()
    text_send("g1", slot_of(2, 0).at[lo], slot_of(2, 1).at[lo], grid_at(0, 1))
    text_send("xyp", slot_of(0, 1), slot_of(3, 1), grid_at(1, 0))
    text_send("xym", slot_of(0, 1), slot_of(1, 1), grid_at(3, 0))
    for n, i in enumerate((1, 3, 2)):
        wd_copies[1 + n].wait_recv()
        to_sibling(2 + n, x_hi * 4 + lax.rem(z + 4 - i, 4))
    for n, i in enumerate((1, 3, 2)):
        wd_copies[4 + n].wait_recv()
        to_sibling(5 + n, (1 - x_hi) * 4 + lax.rem(z + 4 - i, 4))

    loads[0].wait_recv()
    for cp in sib_copies:
        cp.wait_recv()
    def partial(dy, dx, e):
        block = lax.rem(y + dy, 4) * 2 + lax.rem(x + dx, 2)
        return dot(inner[...], wd_all[block * 2 + e])

    def make(dy, dx):
        for e in range(2):
            rs2_send[dy * 2 + dx, :, e * 512 : (e + 1) * 512] = partial(dy, dx, e).astype(BF)

    sums = []

    def sum_send(src, dst, dev):
        n = len(sums)
        sums.append(remote(src, dst, r2_s.at[n], r2_r.at[n], dev))

    def add(slot, part, rows):
        rs2_send[slot, rows, :] = (
            rs2_send[slot, rows, :].astype(F32) + rs2_recv[part, rows, :].astype(F32)
        ).astype(BF)

    top, low = pl.ds(0, 64), pl.ds(64, 64)
    every = pl.ds(0, 128)
    make(2, 1)
    sum_send(rs2_send.at[5], rs2_recv.at[0], grid_at(0, 1))
    make(1, 1)
    sum_send(rs2_send.at[3], rs2_recv.at[1], grid_at(1, 0))
    make(3, 1)
    sum_send(rs2_send.at[7], rs2_recv.at[2], grid_at(3, 0))
    make(2, 0)
    make(0, 1)
    make(1, 0)
    make(3, 0)
    for e in range(2):
        own_part2[:, e * 512 : (e + 1) * 512] = partial(0, 0, e)
    sums[0].wait_recv()
    add(4, 0, every)
    sum_send(rs2_send.at[4, top], rs2_recv.at[3, top], grid_at(1, 0))
    sum_send(rs2_send.at[4, low], rs2_recv.at[3, low], grid_at(3, 0))
    sums[1].wait_recv()
    sums[2].wait_recv()
    add(1, 1, every)
    add(1, 2, every)
    sum_send(rs2_send.at[1], rs2_recv.at[4], grid_at(0, 1))
    sums[3].wait_recv()
    add(2, 3, top)
    sum_send(rs2_send.at[2], rs2_recv.at[5], grid_at(1, 0))
    sums[4].wait_recv()
    add(6, 3, low)
    sum_send(rs2_send.at[6], rs2_recv.at[6], grid_at(3, 0))

    third, last = pl.ds(256, 128), pl.ds(384, 128)
    txt["xyp"].wait_recv()
    text_send("h1", slot_of(3, 1).at[third], slot_of(2, 1).at[third], grid_at(1, 0))
    txt["xym"].wait_recv()
    text_send("h2", slot_of(1, 1).at[last], slot_of(2, 1).at[last], grid_at(3, 0))
    project_text(3, 7)
    for n in ("f2", "g1", "h1", "h2"):
        txt[n].wait_recv()
    project_text(4, 5)

    @pl.loop(0, 4)
    def _(r):
        sl = pl.ds(pl.multiple_of(r * 128, 128), 128)
        inv = inverse(ss_t[sl, :])
        q_text[sl, :] = (acc_t[sl, 0:512] * inv).astype(BF)
        kv_text[0, sl, :] = (acc_t[sl, 512:768] * inv).astype(BF)

    def kt_copy(src, dst, n, dev):
        return pltpu.make_async_remote_copy(
            src_ref=kv_text.at[src], dst_ref=kv_text.at[dst], send_sem=kt_s.at[n], recv_sem=kt_r.at[n],
            device_id=dev, device_id_type=MESH,
        )

    def kt_along(i):
        return kt_copy(0, i, i, z_at(i))

    def kt_on(i):
        return kt_copy(4, 4 - i, 4 + i, z_at(4 - i))

    kt_cross = kt_copy(0, 4, 4, (partner, t, d))

    @pl.when(x_hi == 0)
    def _():
        kt_cross.start()

    for i in range(1, 4):

        @pl.when(z + i < 4)
        def _():
            kt_along(i).start()

    for cp in sums:
        cp.wait_recv()
    total = own_part2[...]
    for i in range(4, 7):
        total += rs2_recv[i].astype(F32)
    vis_all[0] = total.astype(BF)
    vis_at = lambda dy, dx: vis_all.at[dy * 2 + dx]
    vis = {}

    def vis_send(name, src, dst, dev):
        n = len(vis)
        vis[name] = remote(src, dst, vs_s.at[n], vs_r.at[n], dev)

    vis_send("yp", vis_at(0, 0), vis_at(3, 0), grid_at(1, 0))
    vis_send("ym", vis_at(0, 0), vis_at(1, 0), grid_at(3, 0))
    vis_send("x0", vis_at(0, 0), vis_at(0, 1), grid_at(0, 1))
    vis["yp"].wait_recv()
    vis_send("f1", vis_at(3, 0).at[top], vis_at(2, 0).at[top], grid_at(1, 0))
    vis["ym"].wait_recv()
    vis_send("f2", vis_at(1, 0).at[low], vis_at(2, 0).at[low], grid_at(3, 0))
    vis["x0"].wait_recv()
    vis_send("xyp", vis_at(0, 1), vis_at(3, 1), grid_at(1, 0))
    vis_send("xym", vis_at(0, 1), vis_at(1, 1), grid_at(3, 0))
    vis["f1"].wait_recv()
    vis_send("g1", vis_at(2, 0).at[top], vis_at(2, 1).at[top], grid_at(0, 1))
    vis["f2"].wait_recv()
    vis_send("g2", vis_at(2, 0).at[low], vis_at(2, 1).at[low], grid_at(0, 1))

    @pl.when(x_hi == 1)
    def _():
        kt_cross.wait_recv()
        for i in range(1, 4):

            @pl.when(z - i >= 0)
            def _():
                kt_on(i).start()

    for cp in vis.values():
        cp.wait_recv()
    acc_v[...] = jnp.zeros_like(acc_v)
    ss_v[...] = jnp.zeros_like(ss_v)

    @pl.loop(0, 8)
    def _(slot):
        block = lax.rem(y + slot // 2, 4) * 2 + lax.rem(x + lax.rem(slot, 2), 2)
        project(vis_all, slot, block, acc_v, ss_v, 128, 128)

    inv = inverse(ss_v[...])
    kv_own[...] = (acc_v[:, 512:768] * inv).astype(BF)
    kv_copies = []
    for i in range(1, 8):
        kv_copies.append(remote(kv_own, kv_vis.at[c], kv_s.at[i], kv_r.at[i], ctx_at(i)))
    kv_vis[c] = kv_own[...]
    qv = (acc_v[:, 0:512] * inv).astype(BF)
    dest = place_row[...] // 512
    hit = lax.broadcasted_iota(jnp.int32, (8, 128), 0) == dest
    hit_f = hit.astype(F32)
    before = (
        lax.broadcasted_iota(jnp.int32, (128, 128), 0) < lax.broadcasted_iota(jnp.int32, (128, 128), 1)
    ).astype(F32).astype(BF)
    rank = jnp.sum(dot(hit_f.astype(BF), before) * hit_f, axis=0, keepdims=True)
    slot_row = dest * 32 + rank.astype(jnp.int32)
    pick = (lax.broadcasted_iota(jnp.int32, (256, 128), 0) == slot_row).astype(F32).astype(BF)
    slots_out[...] = dot(pick, qv).astype(BF)
    qs_copies = []
    for i in range(1, 8):
        sl = pl.ds(pl.multiple_of(lax.rem(c + i, 8) * 32, 32), 32)
        qs_copies.append(remote(slots_out.at[sl], q_slots.at[c], qs_s.at[i], qs_r.at[i], ctx_at(i)))
    q_slots[c] = slots_out[pl.ds(pl.multiple_of(c * 32, 32), 32), :]

    @pl.when(x_hi == 0)
    def _():
        kt_cross.wait_send()

    for i in range(1, 4):

        @pl.when(z - i >= 0)
        def _():
            kt_along(i).wait_recv()

        @pl.when(z + i < 4)
        def _():
            kt_along(i).wait_send()

        @pl.when((x_hi == 1) & (z + i < 4))
        def _():
            kt_on(i).wait_recv()

        @pl.when((x_hi == 1) & (z - i >= 0))
        def _():
            kt_on(i).wait_send()

    finish()


def attend_kernel(
    q_text, kv_text, q_slots, kv_vis, pos_all, seg_s, segments, out,
    place, expand, q_v, k_v, v_v, m_v, l_v, acc,
):
    c = lax.axis_index("ctx")
    lanes = kv_vis.shape[1]
    own = pl.ds(pl.multiple_of(c * 512, 512), 512)
    pos = pos_all[...]
    hit = (pos // 512) == c
    before = (
        lax.broadcasted_iota(jnp.int32, (128, 128), 0) < lax.broadcasted_iota(jnp.int32, (128, 128), 1)
    ).astype(F32).astype(BF)
    rank = dot(hit.astype(F32).astype(BF), before).astype(jnp.int32)
    slot = jnp.where(hit, rank, -1)
    ones = jnp.ones((1024, 128), BF)

    for s in range(8):
        back = (lax.broadcasted_iota(jnp.int32, (32, lanes), 0) == slot[s : s + 1, :]).astype(F32)
        expand[s * lanes : (s + 1) * lanes, :] = dot(
            jnp.transpose(back).astype(BF), q_slots[s]
        ).astype(BF)
    seg_q = jnp.transpose(jnp.broadcast_to(segments[:, own], (8, 512)))[:, 0:1]
    log2e = 1.4426950408889634

    for j in range(5):
        base = (c - j) * 512
        first = jnp.maximum(base, 0)

        @pl.when((base >= 0) & (seg_s[0, first + 511] == seg_s[0, c * 512]) if j else base >= 0)
        def _():
            rows = lax.broadcasted_iota(jnp.int32, (512, lanes), 0) + base
            for s in range(8):
                place[:, s * lanes : (s + 1) * lanes] = (
                    (rows == pos[s : s + 1, :]).astype(F32).astype(BF)
                )
            is_vis = dot(place[...], ones) > 0.5
            placed = dot(place[...], kv_vis[...].reshape(1024, 256))
            k_v[...] = jnp.where(is_vis, placed[:, 0:128], kv_text[j, :, 0:128].astype(F32)).astype(BF)
            v_v[...] = jnp.where(is_vis, placed[:, 128:256], kv_text[j, :, 128:256].astype(F32)).astype(BF)
            if j == 0:
                placed_q = dot(place[...], expand[...])
                for h in range(4):
                    sl = slice(h * 128, (h + 1) * 128)
                    qh = jnp.where(is_vis, placed_q[:, sl], q_text[:, sl].astype(F32)).astype(BF)
                    for r in range(4):
                        q_v[r, sl, :] = qh[r * 128 : (r + 1) * 128, :]
            seg_k = segments[:, pl.ds(pl.multiple_of(first, 512), 512)]
            for r in range(4):
                wide = (r + 1) * 128 if j == 0 else 512
                allowed = seg_q[r * 128 : (r + 1) * 128] == seg_k[:, 0:wide]
                if j == 0:
                    allowed = allowed & (
                        lax.broadcasted_iota(jnp.int32, (128, wide), 1)
                        <= lax.broadcasted_iota(jnp.int32, (128, wide), 0) + r * 128
                    )
                bias = jnp.where(allowed, 0.0, MASKED)
                s_ = dot_nt(q_v[r], k_v[0:wide, :]) * (HD ** (-0.5) * log2e)
                s_ = (s_.reshape(4, 128, wide) + bias[None]).reshape(512, wide)
                top = jnp.max(s_, axis=-1, keepdims=True)
                if j == 0:
                    w = jnp.exp2(s_ - top)
                    m_v[r] = jnp.broadcast_to(top, (512, 128))
                    l_v[r] = jnp.broadcast_to(jnp.sum(w, axis=-1, keepdims=True), (512, 128))
                    acc[r] = dot(w.astype(BF), v_v[0:wide, :])
                else:
                    old = m_v[r]
                    new = jnp.maximum(old, top)
                    alpha = jnp.exp2(old - new)
                    w = jnp.exp2(s_ - new[:, 0:1])
                    m_v[r] = new
                    l_v[r] = l_v[r] * alpha + jnp.sum(w, axis=-1, keepdims=True)
                    acc[r] = acc[r] * alpha + dot(w.astype(BF), v_v[...])

    for r in range(4):
        for h in range(4):
            sl = slice(h * 128, (h + 1) * 128)
            out[r * 128 : (r + 1) * 128, sl] = (acc[r, sl, :] / l_v[r, sl, :]).astype(BF)


def shards(
    patches, window_ids, vit_gain, vit_qkv, vit_out, merge_gain, merge_up, merge_down,
    text_rows, placeholders, segments, llm_gain, w_query, w_keyval,
):
    vm = pl.BlockSpec(memory_space=pltpu.VMEM)
    hbm = pl.BlockSpec(memory_space=pl.ANY)
    dma = pltpu.SemaphoreType.DMA
    sds = jax.ShapeDtypeStruct
    qkv_t = vit_qkv.transpose(1, 2, 0).reshape(480, 1280)
    encoded = pl.pallas_call(
        encode_kernel,
        out_shape=(
            sds((512, 512), BF), sds((5, 512, 256), BF), sds((8, 32, 512), BF),
            sds((8, 128, 256), BF), sds((8, 128), jnp.int32),
        ),
        in_specs=[vm, vm, vm, vm, vm, vm, hbm, hbm, hbm, vm, vm, hbm, hbm],
        out_specs=(vm, vm, vm, vm, vm),
        scratch_shapes=[
            pltpu.VMEM((8, 512, 1024), BF),
            pltpu.VMEM((5120, 640), BF),
            pltpu.VMEM((16, 640, 512), BF),
            pltpu.VMEM((8192, 512), BF),
            pltpu.VMEM((2, 2048, 128), BF),
            pltpu.VMEM((2048, 128), F32),
            pltpu.VMEM((8192, 256), BF),
            pltpu.VMEM((512, 160), BF),
            pltpu.VMEM((512, 160), BF),
            pltpu.VMEM((512, 160), BF),
            pltpu.VMEM((512, 160), BF),
            pltpu.VMEM((8, 64, 1280), BF),
            pltpu.VMEM((8, 64, 1280), BF),
            pltpu.VMEM((64, 1280), F32),
            pltpu.VMEM((10, 64, 128), F32),
            pltpu.VMEM((128, 5120), BF),
            pltpu.VMEM((128, 640), F32),
            pltpu.VMEM((128, 640), BF),
            pltpu.VMEM((8, 128, 1024), BF),
            pltpu.VMEM((8, 128, 1024), BF),
            pltpu.VMEM((128, 1024), F32),
            pltpu.VMEM((8, 128, 1024), BF),
            pltpu.VMEM((512, 768), F32),
            pltpu.VMEM((512, 128), F32),
            pltpu.VMEM((128, 768), F32),
            pltpu.VMEM((128, 128), F32),
            pltpu.VMEM((256, 512), BF),
            pltpu.VMEM((128, 256), BF),
            dma((6,)), dma((10,)), dma((10,)),
        ] + [dma((9,))] * 20,
        compiler_params=pltpu.CompilerParams(
            collective_id=0, has_side_effects=True, vmem_limit_bytes=63 * 2**20
        ),
    )(
        patches[0], window_ids, vit_gain, qkv_t, vit_out,
        merge_gain, merge_up, merge_down, text_rows[0], placeholders,
        llm_gain, w_query, w_keyval.reshape(16384, 128),
    )
    out = pl.pallas_call(
        attend_kernel,
        out_shape=sds((512, 512), BF),
        in_specs=[vm] * 5 + [pl.BlockSpec(memory_space=pltpu.SMEM), vm],
        out_specs=vm,
        scratch_shapes=[
            pltpu.VMEM((512, 1024), BF),
            pltpu.VMEM((1024, 512), BF),
            pltpu.VMEM((4, 512, 128), BF),
            pltpu.VMEM((512, 128), BF),
            pltpu.VMEM((512, 128), BF),
            pltpu.VMEM((4, 512, 128), F32),
            pltpu.VMEM((4, 512, 128), F32),
            pltpu.VMEM((4, 512, 128), F32),
        ],
        compiler_params=pltpu.CompilerParams(vmem_limit_bytes=60 * 2**20),
    )(*encoded, segments, segments)
    return out[None]


def solution(mesh):
    in_specs = (
        P("dp", "ctx", None),
        P("dp", "ctx"),
        P(),
        P(None, None, "tp"),
        P("tp", None),
        P(),
        P(None, "tp"),
        P("tp", ("ctx", "dp")),
        P("dp", "ctx", "tp"),
        P("dp", "ctx"),
        P("dp", None),
        P(),
        P(None, "tp"),
        P(None, None, "tp"),
    )
    out_specs = P("dp", "ctx", "tp")
    return jax.shard_map(shards, mesh=mesh, in_specs=in_specs, out_specs=out_specs, check_vma=False)
```

```python
import jax
import jax.numpy as jnp
from jax import lax
from jax.experimental import pallas as pl
from jax.experimental.pallas import tpu as pltpu
from jax.sharding import PartitionSpec as P

VHD = 80
HD = 128
EPS = 1e-06
MASKED = -1e30
BF = jnp.bfloat16
F32 = jnp.float32
MESH = pl.DeviceIdType.MESH
NT = (((1,), (1,)), ((), ()))


def dot(a, b):
    return jnp.dot(a, b, preferred_element_type=F32)


def dot_nt(a, b):
    return lax.dot_general(a, b, NT, preferred_element_type=F32)


class Sent:
    def __init__(self, copy):
        self.copy = copy
        self.arrived = False

    def wait_recv(self):
        if not self.arrived:
            self.arrived = True
            self.copy.wait_recv()


def encode_kernel(
    patches, window_row, vit_gain, qkv_t, vit_out, merge_gain, merge_up, merge_down,
    text, place_row, llm_gain, w_query, w_keyval,
    q_text, kv_text, q_slots, kv_vis, pos_all,
    text_all, up_v, wd_all, wq_v, wkv_raw, wkv_f, wkv_v, q_v, k_v, v_v, heads_v,
    rs_send, rs_recv, own_part, merge_f, merged, acc_up, inner,
    rs2_send, rs2_recv, own_part2, vis_all, acc_t, ss_t, acc_v, ss_v, slots_out, kv_own,
    loc, txt_s, txt_r, sib_s, sib_r, rs_s, rs_r, mg_s, mg_r, wd_s, wd_r, r2_s, r2_r,
    vs_s, vs_r, kt_s, kt_r, qs_s, qs_r, kv_s, kv_r, ps_s, ps_r,
):
    c = lax.axis_index("ctx")
    t = lax.axis_index("tp")
    d = lax.axis_index("dp")
    y = t // 2
    x = lax.rem(t, 2)
    started = []

    def tp_at(i):
        return (c, lax.rem(t + i, 8), d)

    def ctx_at(i):
        return (lax.rem(c + i, 8), t, d)

    def grid_at(dy, dx):
        return (c, lax.rem(y + dy, 4) * 2 + lax.rem(x + dx, 2), d)

    sibling = (c, t, 1 - d)

    def remote(src, dst, ssem, rsem, dev):
        cp = pltpu.make_async_remote_copy(
            src_ref=src, dst_ref=dst, send_sem=ssem, recv_sem=rsem, device_id=dev, device_id_type=MESH
        )
        cp.start()
        started.append(Sent(cp))
        return started[-1]

    def finish():
        for cp in started:
            cp.wait_recv()
        for cp in started:
            cp.copy.wait_send()
        for cp in loads:
            cp.wait_recv()

    barrier = pltpu.get_barrier_semaphore()
    for i in range(1, 8):
        pl.semaphore_signal(barrier, inc=1, device_id=tp_at(i), device_id_type=MESH)
        pl.semaphore_signal(barrier, inc=1, device_id=ctx_at(i), device_id_type=MESH)
    pl.semaphore_signal(barrier, inc=1, device_id=sibling, device_id_type=MESH)
    loads = [
        Sent(pltpu.make_async_copy(merge_down, wd_all.at[c * 2 + d], loc.at[0])),
        Sent(pltpu.make_async_copy(merge_up, up_v, loc.at[1])),
        Sent(pltpu.make_async_copy(text, text_all.at[0], loc.at[2])),
        Sent(pltpu.make_async_copy(w_query, wq_v, loc.at[3])),
    ] + [
        Sent(pltpu.make_async_copy(w_keyval.at[pl.ds(k * 2048, 2048)], wkv_raw.at[k % 2], loc.at[4 + k % 2]))
        for k in range(8)
    ]
    for cp in loads[:6]:
        cp.copy.start()
    pl.semaphore_wait(barrier, 15)

    pos_copies = []
    pos_all[pl.ds(c, 1), :] = place_row[...]
    for i in range(1, 8):
        pos_copies.append(
            remote(place_row, pos_all.at[pl.ds(c, 1)], ps_s.at[i], ps_r.at[i], ctx_at(i))
        )

    slot_of = lambda dy, dx: text_all.at[dy * 2 + dx]
    half = text.shape[0] // 2
    lo, hi = pl.ds(0, half), pl.ds(half, half)
    txt = {}

    def text_send(name, src, dst, dev):
        n = len(txt)
        txt[name] = remote(src, dst, txt_s.at[n], txt_r.at[n], dev)

    text_send("x0", text, slot_of(0, 1), grid_at(0, 1))
    text_send("yp", text, slot_of(3, 0), grid_at(1, 0))
    text_send("ym", text, slot_of(1, 0), grid_at(3, 0))

    x_hi = c // 4
    z = lax.rem(c, 4)

    def z_at(i):
        return (x_hi * 4 + lax.rem(z + i, 4), t, d)

    def wd_block(ctx):
        return wd_all.at[ctx * 2 + d]

    partner = lax.rem(c + 4, 8)
    wd_copies = [remote(merge_down, wd_block(c), wd_s.at[0], wd_r.at[0], (partner, t, d))]
    for i in (1, 3, 2):
        wd_copies.append(remote(merge_down, wd_block(c), wd_s.at[i], wd_r.at[i], z_at(i)))
    sib_copies = [remote(merge_down, wd_block(c), sib_s.at[0], sib_r.at[0], sibling)]

    def to_sibling(n, ctx):
        sib_copies.append(remote(wd_block(ctx), wd_block(ctx), sib_s.at[n], sib_r.at[n], sibling))

    rows = patches.shape[0]
    step = 128

    @pl.loop(0, rows // step)
    def _(r):
        sl = pl.ds(pl.multiple_of(r * step, step), step)
        v = patches[sl, :].astype(F32)
        ms = jnp.mean(v * v, axis=-1, keepdims=True)
        n = (v * lax.rsqrt(ms + EPS) * vit_gain[...][None, :]).astype(BF)
        q_v[sl, :] = dot_nt(n, qkv_t[0:160, :]).astype(BF)
        k_v[sl, :] = dot_nt(n, qkv_t[160:320, :]).astype(BF)
        v_v[sl, :] = dot_nt(n, qkv_t[320:480, :]).astype(BF)

    @pl.loop(0, rows // step)
    def _(r):
        sl = pl.ds(pl.multiple_of(r * step, step), step)
        qb = q_v[sl, :]
        col = lax.broadcasted_iota(jnp.int32, (step, 160), 1)
        ids = jnp.transpose(jnp.broadcast_to(window_row[:, sl], (8, step)))[:, 0:1]
        same = ids == window_row[...]
        outs = []
        for h in range(2):
            mine = (col < VHD) if h == 0 else (col >= VHD)
            qh = jnp.where(mine, qb, jnp.zeros_like(qb))
            s = dot_nt(qh, k_v[...]) * VHD ** (-0.5)
            s = jnp.where(same, s, MASKED)
            w = jnp.where(same, jnp.exp(s - jnp.max(s, axis=-1, keepdims=True)), 0.0)
            tot = jnp.sum(w, axis=-1, keepdims=True)
            outs.append(dot(w.astype(BF), v_v[...]) / tot)
        heads_v[sl, :] = jnp.where(col < VHD, outs[0], outs[1]).astype(BF)

    rs_copies = [None]
    for i in list(range(1, 8)) + [0]:
        dst = lax.rem(t + i, 8)
        hb = heads_v[pl.ds(pl.multiple_of(dst * 64, 64), 64), :]
        part = dot(hb, vit_out[...])
        if i == 0:
            own_part[...] = part
        else:
            rs_send[i] = part.astype(BF)
            rs_copies.append(remote(rs_send.at[i], rs_recv.at[i], rs_s.at[i], rs_r.at[i], tp_at(i)))

    for k in range(8):
        loads[4 + k].wait_recv()
        wkv_f[...] = wkv_raw[k % 2].astype(F32)
        if k < 6:
            loads[6 + k].copy.start()
        sl = pl.ds(k * 1024, 1024)
        wkv_v[sl, 0:128] = wkv_f[pl.ds(0, 1024, stride=2), :].astype(BF)
        wkv_v[sl, 128:256] = wkv_f[pl.ds(1, 1024, stride=2), :].astype(BF)

    wd_copies[0].wait_recv()
    for n, i in enumerate((1, 3, 2)):
        wd_copies.append(remote(wd_block(partner), wd_block(partner), wd_s.at[4 + n], wd_r.at[4 + n], z_at(i)))
    to_sibling(1, partner)

    for cp in rs_copies[1:]:
        cp.wait_recv()
    own_rows = pl.ds(pl.multiple_of(t * 64, 64), 64)
    res = patches[own_rows, :].astype(F32) + own_part[...]
    for i in range(1, 8):
        res += rs_recv[i].astype(F32)
    ms = jnp.mean(res * res, axis=-1, keepdims=True)
    res = res * lax.rsqrt(ms + EPS) * merge_gain[...][None, :]
    for b in range(10):
        merge_f[b] = res[:, b * 128 : (b + 1) * 128]
    own_m = pl.ds(pl.multiple_of(t * 16, 16), 16)
    for j in range(4):
        for b in range(10):
            at = j * 1280 + b * 128
            merged[own_m, at : at + 128] = merge_f[b, pl.ds(j, 16, stride=4), :].astype(BF)
    def merged_at(dy, dx, cols=slice(None)):
        block = lax.rem(y + dy, 4) * 2 + lax.rem(x + dx, 2)
        return merged.at[pl.ds(pl.multiple_of(block * 16, 16), 16), cols]

    mrg = {}

    def merged_send(name, ref, dev):
        n = len(mrg)
        mrg[name] = remote(ref, ref, mg_s.at[n], mg_r.at[n], dev)

    left, right = pl.ds(0, 2560), pl.ds(2560, 2560)
    merged_send("yp", merged_at(0, 0), grid_at(1, 0))
    merged_send("ym", merged_at(0, 0), grid_at(3, 0))
    merged_send("x0", merged_at(0, 0), grid_at(0, 1))
    mrg["yp"].wait_recv()
    merged_send("f1", merged_at(3, 0, left), grid_at(1, 0))
    mrg["ym"].wait_recv()
    merged_send("f2", merged_at(1, 0, right), grid_at(3, 0))
    mrg["x0"].wait_recv()
    merged_send("xyp", merged_at(0, 1), grid_at(1, 0))
    merged_send("xym", merged_at(0, 1), grid_at(3, 0))
    mrg["f1"].wait_recv()
    merged_send("g1", merged_at(2, 0, left), grid_at(0, 1))
    mrg["f2"].wait_recv()
    merged_send("g2", merged_at(2, 0, right), grid_at(0, 1))

    loads[2].wait_recv()
    loads[3].wait_recv()
    def project(source, slot, block, acc, ss, row_count, chunk):
        feats = pl.ds(pl.multiple_of(block * 1024, 1024), 1024)
        gain = llm_gain[feats][None, :]

        @pl.loop(0, row_count // chunk)
        def _(r):
            sl = pl.ds(pl.multiple_of(r * chunk, chunk), chunk)
            v = source[slot, sl, :].astype(F32)
            sq = v * v
            part = sq[:, 0:128]
            for j in range(1, 8):
                part += sq[:, j * 128 : (j + 1) * 128]
            ss[sl, :] += part
            xb = (v * gain).astype(BF)
            acc[sl, 0:512] += dot(xb, wq_v[feats, :])
            acc[sl, 512:768] += dot(xb, wkv_v[feats, :])

    def inverse(ss):
        return lax.rsqrt(jnp.sum(ss, axis=-1, keepdims=True) * (1.0 / 8192) + EPS)

    def project_text(first, second):
        @pl.loop(0, 2)
        def _(n):
            slot = jnp.where(n == 0, first, second)
            block = lax.rem(y + slot // 2, 4) * 2 + lax.rem(x + lax.rem(slot, 2), 2)
            project(text_all, slot, block, acc_t, ss_t, 512, 256)

    acc_t[...] = jnp.zeros_like(acc_t)
    ss_t[...] = jnp.zeros_like(ss_t)
    txt["x0"].wait_recv()
    project_text(0, 1)

    for cp in mrg.values():
        cp.wait_recv()
    txt["yp"].wait_recv()
    text_send("f1", slot_of(3, 0).at[lo], slot_of(2, 0).at[lo], grid_at(1, 0))
    txt["ym"].wait_recv()
    text_send("f2", slot_of(1, 0).at[hi], slot_of(2, 0).at[hi], grid_at(3, 0))
    loads[1].wait_recv()
    acc_up[...] = jnp.zeros_like(acc_up)

    @pl.loop(0, 4)
    def _(k):
        sl = pl.ds(pl.multiple_of(k * 1280, 1280), 1280)
        acc_up[...] += dot(merged[:, sl], up_v[sl, :])

    pre = acc_up[...]
    inner[...] = (0.5 * pre * (1.0 + lax.erf(pre * (0.5**0.5)))).astype(BF)

    project_text(2, 6)
    txt["f1"].wait_recv()
    text_send("g1", slot_of(2, 0).at[lo], slot_of(2, 1).at[lo], grid_at(0, 1))
    text_send("xyp", slot_of(0, 1), slot_of(3, 1), grid_at(1, 0))
    text_send("xym", slot_of(0, 1), slot_of(1, 1), grid_at(3, 0))
    for n, i in enumerate((1, 3, 2)):
        wd_copies[1 + n].wait_recv()
        to_sibling(2 + n, x_hi * 4 + lax.rem(z + 4 - i, 4))
    for n, i in enumerate((1, 3, 2)):
        wd_copies[4 + n].wait_recv()
        to_sibling(5 + n, (1 - x_hi) * 4 + lax.rem(z + 4 - i, 4))

    loads[0].wait_recv()
    for cp in sib_copies:
        cp.wait_recv()
    def partial(dy, dx, e):
        block = lax.rem(y + dy, 4) * 2 + lax.rem(x + dx, 2)
        return dot(inner[...], wd_all[block * 2 + e])

    def make(dy, dx):
        for e in range(2):
            rs2_send[dy * 2 + dx, :, e * 512 : (e + 1) * 512] = partial(dy, dx, e).astype(BF)

    sums = []

    def sum_send(src, dst, dev):
        n = len(sums)
        sums.append(remote(src, dst, r2_s.at[n], r2_r.at[n], dev))

    def add(slot, part, rows):
        rs2_send[slot, rows, :] = (
            rs2_send[slot, rows, :].astype(F32) + rs2_recv[part, rows, :].astype(F32)
        ).astype(BF)

    top, low = pl.ds(0, 64), pl.ds(64, 64)
    every = pl.ds(0, 128)
    make(2, 1)
    sum_send(rs2_send.at[5], rs2_recv.at[0], grid_at(0, 1))
    make(1, 1)
    sum_send(rs2_send.at[3], rs2_recv.at[1], grid_at(1, 0))
    make(3, 1)
    sum_send(rs2_send.at[7], rs2_recv.at[2], grid_at(3, 0))
    make(2, 0)
    make(0, 1)
    make(1, 0)
    make(3, 0)
    for e in range(2):
        own_part2[:, e * 512 : (e + 1) * 512] = partial(0, 0, e)
    sums[0].wait_recv()
    add(4, 0, every)
    sum_send(rs2_send.at[4, top], rs2_recv.at[3, top], grid_at(1, 0))
    sum_send(rs2_send.at[4, low], rs2_recv.at[3, low], grid_at(3, 0))
    sums[1].wait_recv()
    sums[2].wait_recv()
    add(1, 1, every)
    add(1, 2, every)
    sum_send(rs2_send.at[1], rs2_recv.at[4], grid_at(0, 1))
    sums[3].wait_recv()
    add(2, 3, top)
    sum_send(rs2_send.at[2], rs2_recv.at[5], grid_at(1, 0))
    sums[4].wait_recv()
    add(6, 3, low)
    sum_send(rs2_send.at[6], rs2_recv.at[6], grid_at(3, 0))

    third, last = pl.ds(256, 128), pl.ds(384, 128)
    txt["xyp"].wait_recv()
    text_send("h1", slot_of(3, 1).at[third], slot_of(2, 1).at[third], grid_at(1, 0))
    txt["xym"].wait_recv()
    text_send("h2", slot_of(1, 1).at[last], slot_of(2, 1).at[last], grid_at(3, 0))
    project_text(3, 7)
    for n in ("f2", "g1", "h1", "h2"):
        txt[n].wait_recv()
    project_text(4, 5)

    @pl.loop(0, 4)
    def _(r):
        sl = pl.ds(pl.multiple_of(r * 128, 128), 128)
        inv = inverse(ss_t[sl, :])
        q_text[sl, :] = (acc_t[sl, 0:512] * inv).astype(BF)
        kv_text[0, sl, :] = (acc_t[sl, 512:768] * inv).astype(BF)

    def kt_copy(src, dst, n, dev):
        return pltpu.make_async_remote_copy(
            src_ref=kv_text.at[src], dst_ref=kv_text.at[dst], send_sem=kt_s.at[n], recv_sem=kt_r.at[n],
            device_id=dev, device_id_type=MESH,
        )

    def kt_along(i):
        return kt_copy(0, i, i, z_at(i))

    def kt_on(i):
        return kt_copy(4, 4 - i, 4 + i, z_at(4 - i))

    kt_cross = kt_copy(0, 4, 4, (partner, t, d))

    @pl.when(x_hi == 0)
    def _():
        kt_cross.start()

    for i in range(1, 4):

        @pl.when(z + i < 4)
        def _():
            kt_along(i).start()

    for cp in sums:
        cp.wait_recv()
    total = own_part2[...]
    for i in range(4, 7):
        total += rs2_recv[i].astype(F32)
    vis_all[0] = total.astype(BF)
    vis_at = lambda dy, dx: vis_all.at[dy * 2 + dx]
    vis = {}

    def vis_send(name, src, dst, dev):
        n = len(vis)
        vis[name] = remote(src, dst, vs_s.at[n], vs_r.at[n], dev)

    vis_send("yp", vis_at(0, 0), vis_at(3, 0), grid_at(1, 0))
    vis_send("ym", vis_at(0, 0), vis_at(1, 0), grid_at(3, 0))
    vis_send("x0", vis_at(0, 0), vis_at(0, 1), grid_at(0, 1))
    vis["yp"].wait_recv()
    vis_send("f1", vis_at(3, 0).at[top], vis_at(2, 0).at[top], grid_at(1, 0))
    vis["ym"].wait_recv()
    vis_send("f2", vis_at(1, 0).at[low], vis_at(2, 0).at[low], grid_at(3, 0))
    vis["x0"].wait_recv()
    vis_send("xyp", vis_at(0, 1), vis_at(3, 1), grid_at(1, 0))
    vis_send("xym", vis_at(0, 1), vis_at(1, 1), grid_at(3, 0))
    vis["f1"].wait_recv()
    vis_send("g1", vis_at(2, 0).at[top], vis_at(2, 1).at[top], grid_at(0, 1))
    vis["f2"].wait_recv()
    vis_send("g2", vis_at(2, 0).at[low], vis_at(2, 1).at[low], grid_at(0, 1))

    @pl.when(x_hi == 1)
    def _():
        kt_cross.wait_recv()
        for i in range(1, 4):

            @pl.when(z - i >= 0)
            def _():
                kt_on(i).start()

    for cp in vis.values():
        cp.wait_recv()
    acc_v[...] = jnp.zeros_like(acc_v)
    ss_v[...] = jnp.zeros_like(ss_v)

    @pl.loop(0, 8)
    def _(slot):
        block = lax.rem(y + slot // 2, 4) * 2 + lax.rem(x + lax.rem(slot, 2), 2)
        project(vis_all, slot, block, acc_v, ss_v, 128, 128)

    inv = inverse(ss_v[...])
    kv_own[...] = (acc_v[:, 512:768] * inv).astype(BF)
    kv_copies = []
    for i in range(1, 8):
        kv_copies.append(remote(kv_own, kv_vis.at[c], kv_s.at[i], kv_r.at[i], ctx_at(i)))
    kv_vis[c] = kv_own[...]
    qv = (acc_v[:, 0:512] * inv).astype(BF)
    dest = place_row[...] // 512
    hit = lax.broadcasted_iota(jnp.int32, (8, 128), 0) == dest
    hit_f = hit.astype(F32)
    before = (
        lax.broadcasted_iota(jnp.int32, (128, 128), 0) < lax.broadcasted_iota(jnp.int32, (128, 128), 1)
    ).astype(F32).astype(BF)
    rank = jnp.sum(dot(hit_f.astype(BF), before) * hit_f, axis=0, keepdims=True)
    slot_row = dest * 32 + rank.astype(jnp.int32)
    pick = (lax.broadcasted_iota(jnp.int32, (256, 128), 0) == slot_row).astype(F32).astype(BF)
    slots_out[...] = dot(pick, qv).astype(BF)
    qs_copies = []
    for i in range(1, 8):
        sl = pl.ds(pl.multiple_of(lax.rem(c + i, 8) * 32, 32), 32)
        qs_copies.append(remote(slots_out.at[sl], q_slots.at[c], qs_s.at[i], qs_r.at[i], ctx_at(i)))
    q_slots[c] = slots_out[pl.ds(pl.multiple_of(c * 32, 32), 32), :]

    @pl.when(x_hi == 0)
    def _():
        kt_cross.wait_send()

    for i in range(1, 4):

        @pl.when(z - i >= 0)
        def _():
            kt_along(i).wait_recv()

        @pl.when(z + i < 4)
        def _():
            kt_along(i).wait_send()

        @pl.when((x_hi == 1) & (z + i < 4))
        def _():
            kt_on(i).wait_recv()

        @pl.when((x_hi == 1) & (z - i >= 0))
        def _():
            kt_on(i).wait_send()

    finish()


def attend_kernel(
    q_text, kv_text, q_slots, kv_vis, pos_all, seg_s, segments, out,
    place, expand, q_v, k_v, v_v, m_v, l_v, acc,
):
    c = lax.axis_index("ctx")
    lanes = kv_vis.shape[1]
    own = pl.ds(pl.multiple_of(c * 512, 512), 512)
    pos = pos_all[...]
    hit = (pos // 512) == c
    before = (
        lax.broadcasted_iota(jnp.int32, (128, 128), 0) < lax.broadcasted_iota(jnp.int32, (128, 128), 1)
    ).astype(F32).astype(BF)
    rank = dot(hit.astype(F32).astype(BF), before).astype(jnp.int32)
    slot = jnp.where(hit, rank, -1)
    ones = jnp.ones((1024, 128), BF)

    for s in range(8):
        back = (lax.broadcasted_iota(jnp.int32, (32, lanes), 0) == slot[s : s + 1, :]).astype(F32)
        expand[s * lanes : (s + 1) * lanes, :] = dot(
            jnp.transpose(back).astype(BF), q_slots[s]
        ).astype(BF)
    seg_q = jnp.transpose(jnp.broadcast_to(segments[:, own], (8, 512)))[:, 0:1]
    log2e = 1.4426950408889634

    for j in range(5):
        base = (c - j) * 512
        first = jnp.maximum(base, 0)

        @pl.when((base >= 0) & (seg_s[0, first + 511] == seg_s[0, c * 512]) if j else base >= 0)
        def _():
            rows = lax.broadcasted_iota(jnp.int32, (512, lanes), 0) + base
            for s in range(8):
                place[:, s * lanes : (s + 1) * lanes] = (
                    (rows == pos[s : s + 1, :]).astype(F32).astype(BF)
                )
            is_vis = dot(place[...], ones) > 0.5
            placed = dot(place[...], kv_vis[...].reshape(1024, 256))
            k_v[...] = jnp.where(is_vis, placed[:, 0:128], kv_text[j, :, 0:128].astype(F32)).astype(BF)
            v_v[...] = jnp.where(is_vis, placed[:, 128:256], kv_text[j, :, 128:256].astype(F32)).astype(BF)
            if j == 0:
                placed_q = dot(place[...], expand[...])
                for h in range(4):
                    sl = slice(h * 128, (h + 1) * 128)
                    qh = jnp.where(is_vis, placed_q[:, sl], q_text[:, sl].astype(F32)).astype(BF)
                    for r in range(4):
                        q_v[r, sl, :] = qh[r * 128 : (r + 1) * 128, :]
            seg_k = segments[:, pl.ds(pl.multiple_of(first, 512), 512)]
            def rows_of(r):
                wide = (r + 1) * 128 if j == 0 else 512
                allowed = seg_q[r * 128 : (r + 1) * 128] == seg_k[:, 0:wide]
                if j == 0:
                    allowed = allowed & (
                        lax.broadcasted_iota(jnp.int32, (128, wide), 1)
                        <= lax.broadcasted_iota(jnp.int32, (128, wide), 0) + r * 128
                    )
                bias = jnp.where(allowed, 0.0, MASKED)
                s_ = dot_nt(q_v[r], k_v[0:wide, :]) * (HD ** (-0.5) * log2e)
                s_ = (s_.reshape(4, 128, wide) + bias[None]).reshape(512, wide)
                top = jnp.max(s_, axis=-1, keepdims=True)
                if j == 0:
                    w = jnp.exp2(s_ - top)
                    m_v[r] = jnp.broadcast_to(top, (512, 128))
                    l_v[r] = jnp.broadcast_to(jnp.sum(w, axis=-1, keepdims=True), (512, 128))
                    acc[r] = dot(w.astype(BF), v_v[0:wide, :])
                else:
                    old = m_v[r]
                    new = jnp.maximum(old, top)
                    alpha = jnp.exp2(old - new)
                    w = jnp.exp2(s_ - new[:, 0:1])
                    m_v[r] = new
                    l_v[r] = l_v[r] * alpha + jnp.sum(w, axis=-1, keepdims=True)
                    acc[r] = acc[r] * alpha + dot(w.astype(BF), v_v[...])

            for r in range(4):
                if j == 0:
                    rows_of(r)
                else:
                    pl.when(seg_s[0, first + 511] == seg_s[0, c * 512 + r * 128])(lambda r=r: rows_of(r))

    for r in range(4):
        for h in range(4):
            sl = slice(h * 128, (h + 1) * 128)
            out[r * 128 : (r + 1) * 128, sl] = (acc[r, sl, :] / l_v[r, sl, :]).astype(BF)


def shards(
    patches, window_ids, vit_gain, vit_qkv, vit_out, merge_gain, merge_up, merge_down,
    text_rows, placeholders, segments, llm_gain, w_query, w_keyval,
):
    vm = pl.BlockSpec(memory_space=pltpu.VMEM)
    hbm = pl.BlockSpec(memory_space=pl.ANY)
    dma = pltpu.SemaphoreType.DMA
    sds = jax.ShapeDtypeStruct
    qkv_t = vit_qkv.transpose(1, 2, 0).reshape(480, 1280)
    encoded = pl.pallas_call(
        encode_kernel,
        out_shape=(
            sds((512, 512), BF), sds((5, 512, 256), BF), sds((8, 32, 512), BF),
            sds((8, 128, 256), BF), sds((8, 128), jnp.int32),
        ),
        in_specs=[vm, vm, vm, vm, vm, vm, hbm, hbm, hbm, vm, vm, hbm, hbm],
        out_specs=(vm, vm, vm, vm, vm),
        scratch_shapes=[
            pltpu.VMEM((8, 512, 1024), BF),
            pltpu.VMEM((5120, 640), BF),
            pltpu.VMEM((16, 640, 512), BF),
            pltpu.VMEM((8192, 512), BF),
            pltpu.VMEM((2, 2048, 128), BF),
            pltpu.VMEM((2048, 128), F32),
            pltpu.VMEM((8192, 256), BF),
            pltpu.VMEM((512, 160), BF),
            pltpu.VMEM((512, 160), BF),
            pltpu.VMEM((512, 160), BF),
            pltpu.VMEM((512, 160), BF),
            pltpu.VMEM((8, 64, 1280), BF),
            pltpu.VMEM((8, 64, 1280), BF),
            pltpu.VMEM((64, 1280), F32),
            pltpu.VMEM((10, 64, 128), F32),
            pltpu.VMEM((128, 5120), BF),
            pltpu.VMEM((128, 640), F32),
            pltpu.VMEM((128, 640), BF),
            pltpu.VMEM((8, 128, 1024), BF),
            pltpu.VMEM((8, 128, 1024), BF),
            pltpu.VMEM((128, 1024), F32),
            pltpu.VMEM((8, 128, 1024), BF),
            pltpu.VMEM((512, 768), F32),
            pltpu.VMEM((512, 128), F32),
            pltpu.VMEM((128, 768), F32),
            pltpu.VMEM((128, 128), F32),
            pltpu.VMEM((256, 512), BF),
            pltpu.VMEM((128, 256), BF),
            dma((6,)), dma((10,)), dma((10,)),
        ] + [dma((9,))] * 20,
        compiler_params=pltpu.CompilerParams(
            collective_id=0, has_side_effects=True, vmem_limit_bytes=63 * 2**20
        ),
    )(
        patches[0], window_ids, vit_gain, qkv_t, vit_out,
        merge_gain, merge_up, merge_down, text_rows[0], placeholders,
        llm_gain, w_query, w_keyval.reshape(16384, 128),
    )
    out = pl.pallas_call(
        attend_kernel,
        out_shape=sds((512, 512), BF),
        in_specs=[vm] * 5 + [pl.BlockSpec(memory_space=pltpu.SMEM), vm],
        out_specs=vm,
        scratch_shapes=[
            pltpu.VMEM((512, 1024), BF),
            pltpu.VMEM((1024, 512), BF),
            pltpu.VMEM((4, 512, 128), BF),
            pltpu.VMEM((512, 128), BF),
            pltpu.VMEM((512, 128), BF),
            pltpu.VMEM((4, 512, 128), F32),
            pltpu.VMEM((4, 512, 128), F32),
            pltpu.VMEM((4, 512, 128), F32),
        ],
        compiler_params=pltpu.CompilerParams(vmem_limit_bytes=60 * 2**20),
    )(*encoded, segments, segments)
    return out[None]


def solution(mesh):
    in_specs = (
        P("dp", "ctx", None),
        P("dp", "ctx"),
        P(),
        P(None, None, "tp"),
        P("tp", None),
        P(),
        P(None, "tp"),
        P("tp", ("ctx", "dp")),
        P("dp", "ctx", "tp"),
        P("dp", "ctx"),
        P("dp", None),
        P(),
        P(None, "tp"),
        P(None, None, "tp"),
    )
    out_specs = P("dp", "ctx", "tp")
    return jax.shard_map(shards, mesh=mesh, in_specs=in_specs, out_specs=out_specs, check_vma=False)
```
